32 devices in a mesh: blk: 8 (over z, x), dp: 4 (over y, core).
Axes of the slice: x: 2, y: 2, z: 4, core: 2. Of those that a mesh axis runs over, the one named last changes fastest.
Arguments:
- tokens_in: bfloat16 [32768, 384], P(('blk', 'dp')), may hold values from -6 to 6
- condition: float32 [128, 384], P(('blk', 'dp')), may hold values from -6 to 6
- grad_output: bfloat16 [32768, 384], P(('blk', 'dp')), may hold values from -6 to 6
- expert_ids: int32 [32768, 2], P(('blk', 'dp')), may hold values from 0 to 7, as said below
- slot_rows: int32 [32768, 2], P(('blk', 'dp')), may hold values from 0 to 2559, as said below
- expert_counts: int32 [32, 8], P(('blk', 'dp')), may hold values from 1 to 1023, as said below
- ada_weight: float32 [384, 2304], P('blk', 'dp'), may hold values from -0.3125 to 0.3125
- ada_moment: float32 [384, 2304], P('blk', 'dp'), may hold values from -512 to 512
- qkv_weight: float32 [384, 1152], P('blk', 'dp'), may hold values from -0.3125 to 0.3125
- qkv_moment: float32 [384, 1152], P('blk', 'dp'), may hold values from -512 to 512
- out_weight: float32 [384, 384], P('blk', 'dp'), may hold values from -2.5 to 2.5
- out_moment: float32 [384, 384], P('blk', 'dp'), may hold values from -256 to 256
- router_weight: float32 [384, 8], P('blk', 'dp'), may hold values from -0.15625 to 0.15625
- router_moment: float32 [384, 8], P('blk', 'dp'), may hold values from -1536 to 1536
- shared_up: float32 [2, 384, 1536], P(None, 'blk', 'dp'), may hold values from -0.3125 to 0.3125
- shared_up_moment: float32 [2, 384, 1536], P(None, 'blk', 'dp'), may hold values from -224 to 224
- shared_down: float32 [2, 384, 1536], P(None, 'blk', 'dp'), may hold values from -0.15625 to 0.15625
- shared_down_moment: float32 [2, 384, 1536], P(None, 'blk', 'dp'), may hold values from -448 to 448
- expert_up: float32 [8, 384, 1536], P('blk', None, 'dp'), may hold values from -0.3125 to 0.3125
- expert_up_moment: float32 [8, 384, 1536], P('blk', None, 'dp'), may hold values from -56 to 56
- expert_down: float32 [8, 384, 1536], P('blk', None, 'dp'), may hold values from -0.15625 to 0.15625
- expert_down_moment: float32 [8, 384, 1536], P('blk', None, 'dp'), may hold values from -112 to 112
Outputs:
- block_out: bfloat16 [32768, 384], P(('blk', 'dp'))
- grad_tokens: float32 [32768, 384], P(('blk', 'dp'))
- grad_condition: float32 [128, 384], P(('blk', 'dp'))
- ada_grad: float32 [384, 2304], P('blk', 'dp')
- ada_moment_new: float32 [384, 2304], P('blk', 'dp')
- ada_new: float32 [384, 2304], P('blk', 'dp')
- ada_low: bfloat16 [384, 2304], P('blk', 'dp')
- qkv_grad: float32 [384, 1152], P('blk', 'dp')
- qkv_moment_new: float32 [384, 1152], P('blk', 'dp')
- qkv_new: float32 [384, 1152], P('blk', 'dp')
- qkv_low: bfloat16 [384, 1152], P('blk', 'dp')
- out_grad: float32 [384, 384], P('blk', 'dp')
- out_moment_new: float32 [384, 384], P('blk', 'dp')
- out_new: float32 [384, 384], P('blk', 'dp')
- out_low: bfloat16 [384, 384], P('blk', 'dp')
- router_grad: float32 [384, 8], P('blk', 'dp')
- router_moment_new: float32 [384, 8], P('blk', 'dp')
- router_new: float32 [384, 8], P('blk', 'dp')
- router_low: bfloat16 [384, 8], P('blk', 'dp')
- shared_up_grad: float32 [2, 384, 1536], P(None, 'blk', 'dp')
- shared_up_moment_new: float32 [2, 384, 1536], P(None, 'blk', 'dp')
- shared_up_new: float32 [2, 384, 1536], P(None, 'blk', 'dp')
- shared_up_low: bfloat16 [2, 384, 1536], P(None, 'blk', 'dp')
- shared_down_grad: float32 [2, 384, 1536], P(None, 'blk', 'dp')
- shared_down_moment_new: float32 [2, 384, 1536], P(None, 'blk', 'dp')
- shared_down_new: float32 [2, 384, 1536], P(None, 'blk', 'dp')
- shared_down_low: bfloat16 [2, 384, 1536], P(None, 'blk', 'dp')
- expert_up_grad: float32 [8, 384, 1536], P('blk', None, 'dp')
- expert_up_moment_new: float32 [8, 384, 1536], P('blk', None, 'dp')
- expert_up_new: float32 [8, 384, 1536], P('blk', None, 'dp')
- expert_up_low: bfloat16 [8, 384, 1536], P('blk', None, 'dp')
- expert_down_grad: float32 [8, 384, 1536], P('blk', None, 'dp')
- expert_down_moment_new: float32 [8, 384, 1536], P('blk', None, 'dp')
- expert_down_new: float32 [8, 384, 1536], P('blk', None, 'dp')
- expert_down_low: bfloat16 [8, 384, 1536], P('blk', None, 'dp')
The draws below stay inside these ranges and needn't reach their ends.
Inputs may be any that keep to these rules, and one draw needn't show every extreme that they name: The two experts of a token differ. expert_counts[d, e] is how many choices of the tokens of device d (devices in the order blk+dp, 1024 tokens each) name expert e, so each row sums to 2048. `expert_ids`: each token names two different experts. slot_rows[t, j] is the row of token t's choice j in a buffer of 20 blocks of 128 rows of its device; expert e takes ceil(expert_counts[d, e] / 128) consecutive blocks, the experts' blocks stand in expert order and take all 20 blocks, the rows of an expert are distinct and fill the end of its blocks.
All inputs are finite; a program needn't handle non-finite values.
Results may differ from the reference program's by a relative error of at most 0.013.
The reference program's roundings to bfloat16 on the way count: a program that leaves them out, or rounds other values in their place, can miss the bound.
Values may be sent and summed in bfloat16 or wider, within the bound.
No kernel may reach another device: no remote copies, remote signals or barrier semaphores. Data moves between devices by JAX's collectives and lax.ppermute only.
A program may use at most 320 MiB of HBM per device.

```python
import math
import jax
import jax.numpy as jnp
from jax import lax

D = 384
HEADS = 6
HD = 64
FF = 1536
SHARED = 2
SEQ = 256
BLOCK = 128
NS_STEPS = 5
EXPERTS = 8
TOK_DEV = 1024
BLOCKS_DEV = 20
IMAGES = 128
TOKENS = 32768
DEVICES = 32


def routing_tables(key):
    device_keys = jax.random.split(key, DEVICES)
    chosen = jax.random.randint(jax.random.fold_in(key, 977), (), 0, DEVICES)
    largest = TOK_DEV // BLOCK
    spare = largest - EXPERTS // 2 + 1
    others = EXPERTS - 1

    def one_device(device_key, device):
        order_key, pair_key, token_key, flip_key = jax.random.split(device_key, 4)
        order = jax.random.permutation(order_key, EXPERTS)
        rank = jnp.zeros((EXPERTS,), jnp.int32).at[order].set(jnp.arange(EXPERTS, dtype=jnp.int32))
        extra = spare // others + (rank - 1 < spare % others).astype(jnp.int32)
        blocks = jnp.where(rank == 0, largest, 1 + extra)
        pair_cut = jax.random.randint(pair_key, (EXPERTS // 2,), 1, BLOCK)
        pair_cut = pair_cut.at[0].set(jnp.where(device == chosen, 1, pair_cut[0]))
        cut = pair_cut[rank // 2]
        spaces = jnp.where(rank % 2 == 0, cut, BLOCK - cut)
        counts = BLOCK * blocks - spaces
        count_end = jnp.cumsum(counts)
        count_start = count_end - counts
        block_end = jnp.cumsum(blocks)
        position = jnp.arange(2 * TOK_DEV, dtype=jnp.int32)
        expert = jnp.sum((position[:, None] >= count_end[None, :]).astype(jnp.int32), axis=1)
        slot = block_end[expert] * BLOCK - counts[expert] + position - count_start[expert]
        shuffled = jax.random.permutation(token_key, TOK_DEV)
        flips = jax.random.randint(flip_key, (TOK_DEV,), 0, 2)
        owner = shuffled[position % TOK_DEV]
        column = (position // TOK_DEV + flips[position % TOK_DEV]) % 2
        ids = jnp.zeros((TOK_DEV, 2), jnp.int32).at[owner, column].set(expert)
        slots = jnp.zeros((TOK_DEV, 2), jnp.int32).at[owner, column].set(slot)
        return (ids, slots, counts)
    ids, slots, counts = jax.vmap(one_device)(device_keys, jnp.arange(DEVICES, dtype=jnp.int32))
    return (ids.reshape(TOKENS, 2), slots.reshape(TOKENS, 2), counts)


def draw_expert_ids(key, part):
    tables = routing_tables(key)
    return tables[0]


def draw_slot_rows(key, part):
    tables = routing_tables(key)
    return tables[1]


def draw_expert_counts(key, part):
    tables = routing_tables(key)
    return tables[2]


def block_scale(own_key, extent, cuts, least, high):
    gain, own = 1.0, jax.random.fold_in(own_key, 6)
    for axis_at, parts in cuts:
        draws = jnp.exp(jax.random.uniform(jax.random.fold_in(own, axis_at), (parts,), jnp.float32, least / len(cuts), high / len(cuts)))
        gain = gain * jnp.repeat(draws, extent[axis_at] // parts).reshape([-1 if axis == axis_at else 1 for axis in range(len(extent))])
    return gain


def scatter_about(own_key, extent, spread, most, shards=(), held_as=jnp.bfloat16):
    factor_of = block_scale(own_key, extent, shards, -0.22, 0.18) if shards else 1.0
    values = jax.random.normal(own_key, extent, jnp.float32) * spread * factor_of
    return jnp.minimum(jnp.maximum(values, -most), most).astype(held_as)


def setup_inputs(seed: int = 0) -> dict:
    arg_keys = jax.random.split(jax.random.key(seed), 23)
    return {
        "tokens_in": scatter_about(arg_keys[0], (TOKENS, D), 1.0, 6.0, ((0, 32),)),
        "condition": scatter_about(arg_keys[1], (IMAGES, D), 1.0, 6.0, ((0, 32),), jnp.float32),
        "grad_output": scatter_about(arg_keys[2], (TOKENS, D), 1.0, 6.0, ((0, 32),)),
        "expert_ids": draw_expert_ids(jax.random.fold_in(arg_keys[22], 71), 0),
        "slot_rows": draw_slot_rows(jax.random.fold_in(arg_keys[22], 71), 0),
        "expert_counts": draw_expert_counts(jax.random.fold_in(arg_keys[22], 71), 0),
        "ada_weight": scatter_about(arg_keys[6], (D, 6 * D), D ** -0.5, 0.3125, ((0, 8), (1, 4)), jnp.float32),
        "ada_moment": scatter_about(arg_keys[7], (D, 6 * D), (0.5 * TOKENS ** 0.5), 512.0, ((0, 8), (1, 4)), jnp.float32),
        "qkv_weight": scatter_about(arg_keys[8], (D, 3 * D), D ** -0.5, 0.3125, ((0, 8), (1, 4)), jnp.float32),
        "qkv_moment": scatter_about(arg_keys[9], (D, 3 * D), (0.5 * TOKENS ** 0.5), 512.0, ((0, 8), (1, 4)), jnp.float32),
        "out_weight": scatter_about(arg_keys[10], (D, D), (D // 64) ** -0.5, 2.5, ((0, 8), (1, 4)), jnp.float32),
        "out_moment": scatter_about(arg_keys[11], (D, D), (0.25 * TOKENS ** 0.5), 256.0, ((0, 8), (1, 4)), jnp.float32),
        "router_weight": scatter_about(arg_keys[12], (D, EXPERTS), (4 * D) ** -0.5, 0.15625, ((0, 8), (1, 4)), jnp.float32),
        "router_moment": scatter_about(arg_keys[13], (D, EXPERTS), (0.15 * (2 * D * TOKENS // EXPERTS) ** 0.5), 1536.0, ((0, 8), (1, 4)), jnp.float32),
        "shared_up": scatter_about(arg_keys[14], (SHARED, D, FF), D ** -0.5, 0.3125, ((1, 8), (2, 4)), jnp.float32),
        "shared_up_moment": scatter_about(arg_keys[15], (SHARED, D, FF), (0.2 * TOKENS ** 0.5), 224.0, ((1, 8), (2, 4)), jnp.float32),
        "shared_down": scatter_about(arg_keys[16], (SHARED, D, FF), FF ** -0.5, 0.15625, ((1, 8), (2, 4)), jnp.float32),
        "shared_down_moment": scatter_about(arg_keys[17], (SHARED, D, FF), (0.4 * TOKENS ** 0.5), 448.0, ((1, 8), (2, 4)), jnp.float32),
        "expert_up": scatter_about(arg_keys[18], (EXPERTS, D, FF), D ** -0.5, 0.3125, ((0, 8), (2, 4)), jnp.float32),
        "expert_up_moment": scatter_about(arg_keys[19], (EXPERTS, D, FF), (0.1 * (2 * TOKENS // EXPERTS) ** 0.5), 56.0, ((0, 8), (2, 4)), jnp.float32),
        "expert_down": scatter_about(arg_keys[20], (EXPERTS, D, FF), FF ** -0.5, 0.15625, ((0, 8), (2, 4)), jnp.float32),
        "expert_down_moment": scatter_about(arg_keys[21], (EXPERTS, D, FF), (0.2 * (2 * TOKENS // EXPERTS) ** 0.5), 112.0, ((0, 8), (2, 4)), jnp.float32),
    }


@jax.custom_vjp
def low(v):
    return lax.optimization_barrier(v.astype(jnp.bfloat16)).astype(jnp.float32)

@jax.custom_vjp
def low_back(v):
    return v

def low_keep(v):
    return (low(v), None)

def low_pass(kept, grad):
    return (grad,)

def back_keep(v):
    return (v, None)

def back_low(kept, grad):
    return (low(grad),)
low.defvjp(low_keep, low_pass)
low_back.defvjp(back_keep, back_low)
linear_term = 3.4445
cubic_term = -4.775
quintic_term = 2.0315

def precise(left, right):
    return jnp.dot(left, right, precision=lax.Precision.HIGHEST)

def gelu_tanh(values):
    return jax.nn.gelu(values, approximate=True)

def layer_norm(values):
    average = lax.optimization_barrier(jnp.mean(values, axis=-1, keepdims=True))
    centred = values - average
    return centred * lax.rsqrt(lax.optimization_barrier(jnp.mean(centred * centred, axis=-1, keepdims=True)) + 1e-06)

def attention_group(group_in, modulation, qkv_matrix, out_matrix):
    count = group_in.shape[0]
    shift = modulation[:, 0][:, None]
    scale = modulation[:, 1][:, None]
    gate = modulation[:, 2][:, None]
    normed = low(layer_norm(group_in) * (1.0 + scale) + shift)
    packed = low(low_back(jnp.einsum('gsd,de->gse', normed, qkv_matrix, precision=lax.Precision.HIGHEST)))
    packed = packed.reshape(count, SEQ, 3, HEADS, HD)
    queries = packed[:, :, 0]
    keys = packed[:, :, 1]
    values = packed[:, :, 2]
    scores = low_back(jnp.einsum('gqhd,gkhd->ghqk', queries, keys, precision=lax.Precision.HIGHEST) * HD ** (-0.5))
    weights = low(jax.nn.softmax(scores, axis=-1))
    mixed = low(low_back(jnp.einsum('ghqk,gkhd->gqhd', weights, values, precision=lax.Precision.HIGHEST)))
    branch = low_back(jnp.einsum('gqe,ed->gqd', mixed.reshape(count, SEQ, D), out_matrix, precision=lax.Precision.HIGHEST))
    return group_in + gate * branch

def shared_group(rows, up_stack, down_stack):
    total = jnp.zeros(rows.shape, jnp.float32)
    for member in range(SHARED):
        pre = low_back(precise(rows, up_stack[member]))
        hidden = low(gelu_tanh(pre))
        total = total + low_back(lax.dot_general(hidden, down_stack[member], (((1,), (1,)), ((), ())), precision=lax.Precision.HIGHEST))
    return total

def expert_block(rows, expert, up_stack, down_stack):
    up_matrix = lax.dynamic_index_in_dim(up_stack, expert, 0, keepdims=False)
    down_matrix = lax.dynamic_index_in_dim(down_stack, expert, 0, keepdims=False)
    pre = low_back(precise(rows, up_matrix))
    hidden = low(gelu_tanh(pre))
    return low_back(lax.dot_general(hidden, down_matrix, (((1,), (1,)), ((), ())), precision=lax.Precision.HIGHEST))

def source_rows(slots_device):
    flat = slots_device.reshape(-1)
    owners = jnp.repeat(jnp.arange(TOK_DEV, dtype=jnp.int32), 2)
    return jnp.full((BLOCKS_DEV * BLOCK,), TOK_DEV, jnp.int32).at[flat].set(owners)

def orthogonal(matrix):
    current = matrix / (jnp.sqrt(jnp.sum(matrix * matrix)) + 1e-07)
    for iteration in range(NS_STEPS):
        gram = lax.dot_general(current, current, (((1,), (1,)), ((), ())), precision=lax.Precision.HIGHEST)
        mixer = cubic_term * gram + quintic_term * precise(gram, gram)
        current = linear_term * current + precise(mixer, current)
    return current

def orthogonalize(matrix):
    if matrix.shape[0] > matrix.shape[1]:
        return orthogonal(matrix.T).T
    return orthogonal(matrix)

def reference(tokens_in, condition, grad_output, expert_ids, slot_rows, expert_counts, ada_weight, ada_moment, qkv_weight, qkv_moment, out_weight, out_moment, router_weight, router_moment, shared_up, shared_up_moment, shared_down, shared_down_moment, expert_up, expert_up_moment, expert_down, expert_down_moment):
    masters = (ada_weight, qkv_weight, out_weight, router_weight, shared_up, shared_down, expert_up, expert_down)
    moments = (ada_moment, qkv_moment, out_moment, router_moment, shared_up_moment, shared_down_moment, expert_up_moment, expert_down_moment)
    copies = tuple((master.astype(jnp.bfloat16).astype(jnp.float32) for master in masters))
    image_group = math.gcd(IMAGES, max(1, 4096 // SEQ))
    token_group = math.gcd(TOKENS, 4096)
    slots_device = slot_rows.reshape(DEVICES, TOK_DEV, 2)
    sources = jax.vmap(source_rows)(slots_device)
    block_counts = (expert_counts + BLOCK - 1) // BLOCK
    block_end = jnp.cumsum(block_counts, axis=1)
    block_places = jnp.arange(BLOCKS_DEV, dtype=jnp.int32)
    block_expert = lax.optimization_barrier(jnp.sum((block_places[None, :, None] >= block_end[:, None, :]).astype(jnp.int32), axis=2))

    def forward(tokens, conditioning, ada_matrix, qkv_matrix, out_matrix, router_matrix, shared_ups, shared_downs, expert_ups, expert_downs):
        modulation = precise(low(jax.nn.silu(conditioning)), ada_matrix).reshape(IMAGES, 6, D)
        groups = IMAGES // image_group
        attended = lax.map(jax.checkpoint(lambda pair: attention_group(pair[0], pair[1], qkv_matrix, out_matrix)), (tokens.reshape(groups, image_group, SEQ, D), modulation[:, 0:3].reshape(groups, image_group, 3, D)))
        middle = attended.reshape(IMAGES, SEQ, D)
        moe_in = low(layer_norm(middle) * (1.0 + modulation[:, 4][:, None]) + modulation[:, 3][:, None]).reshape(TOKENS, D)
        logits = low_back(precise(moe_in, router_matrix))
        gates = jax.nn.softmax(jnp.take_along_axis(logits, expert_ids, axis=1), axis=1)
        shared_out = lax.map(jax.checkpoint(lambda rows: shared_group(rows, shared_ups, shared_downs)), moe_in.reshape(TOKENS // token_group, token_group, D)).reshape(TOKENS, D)
        padded = jnp.concatenate([moe_in.reshape(DEVICES, TOK_DEV, D), jnp.zeros((DEVICES, 1, D), jnp.float32)], axis=1)
        buffer_in = jax.vmap(lambda rows, picks: rows[picks])(padded, sources)
        routed = lax.map(jax.checkpoint(lambda pair: expert_block(pair[0], pair[1], expert_ups, expert_downs)), (buffer_in.reshape(DEVICES * BLOCKS_DEV, BLOCK, D), block_expert.reshape(DEVICES * BLOCKS_DEV)))
        routed = routed.reshape(DEVICES, BLOCKS_DEV * BLOCK, D)
        first = jax.vmap(lambda rows, picks: rows[picks])(routed, slots_device[:, :, 0]).reshape(TOKENS, D)
        second = jax.vmap(lambda rows, picks: rows[picks])(routed, slots_device[:, :, 1]).reshape(TOKENS, D)
        moe = gates[:, 0:1] * first + gates[:, 1:2] * second + shared_out
        return (middle + modulation[:, 5][:, None] * moe.reshape(IMAGES, SEQ, D)).reshape(TOKENS, D)
    block_value, pullback = jax.vjp(forward, tokens_in.astype(jnp.float32), condition, *copies)
    grads = pullback(grad_output.astype(jnp.float32))
    rates = (math.sqrt(6.0), math.sqrt(3.0), math.sqrt(D / (D // 64)), 0.5, math.sqrt(FF / D), 1.0, math.sqrt(FF / D), 1.0)
    updates = []
    for place in range(8):
        gradient = grads[place + 2]
        moment_new = 0.5 * moments[place] + gradient
        if moment_new.ndim == 3:
            direction = jax.vmap(orthogonalize)(moment_new)
        else:
            direction = orthogonalize(moment_new)
        weight_new = masters[place] - rates[place] * direction
        updates.append((gradient, moment_new, weight_new, weight_new.astype(jnp.bfloat16)))
    return (block_value.astype(jnp.bfloat16), grads[0], grads[1], updates[0][0], updates[0][1], updates[0][2], updates[0][3], updates[1][0], updates[1][1], updates[1][2], updates[1][3], updates[2][0], updates[2][1], updates[2][2], updates[2][3], updates[3][0], updates[3][1], updates[3][2], updates[3][3], updates[4][0], updates[4][1], updates[4][2], updates[4][3], updates[5][0], updates[5][1], updates[5][2], updates[5][3], updates[6][0], updates[6][1], updates[6][2], updates[6][3], updates[7][0], updates[7][1], updates[7][2], updates[7][3])
```

```python
import functools
import math

import jax
import jax.numpy as jnp
from jax import lax
from jax.experimental import pallas as pl
from jax.experimental.pallas import tpu as pltpu
from jax.sharding import PartitionSpec as P

D = 384
HEADS = 6
HD = 64
FF = 1536
SHARED = 2
SEQ = 256
BLOCK = 128
NS_STEPS = 5
ROWS = 256
TP = 2

linear_term = 3.4445
cubic_term = -4.775
quintic_term = 2.0315

bf16 = jnp.bfloat16
f32 = jnp.float32
VMEM_LIMIT = 24 * 1024 * 1024
EXPERT_VMEM = 18 * 1024 * 1024
LANES = 128
WIDE = 2 * D + LANES
COST_UNIT = 0.25e9


def swap(values, axis, mask):
    count = lax.axis_size(axis)
    return lax.ppermute(values, axis, [(i, i ^ mask) for i in range(count)])


def bits(axis):
    count = lax.axis_size(axis)
    return [1 << i for i in range(count.bit_length() - 1)]


def double(values, axis, masks):
    offsets = [0]
    values = values[None]
    for mask in masks:
        values = jnp.concatenate([values, swap(values, axis, mask)], axis=0)
        offsets = offsets + [o ^ mask for o in offsets]
    return values, offsets


def in_order(values, offsets, axis):
    me = lax.axis_index(axis)
    values = jnp.stack([values[offsets.index(j)] for j in range(len(offsets))])
    for mask in bits(axis):
        flipped = jnp.stack([values[j ^ mask] for j in range(len(offsets))])
        values = jnp.where((me & mask) != 0, flipped, values)
    return values


def by_offset(values, axis):
    return in_order(values, list(range(values.shape[0])), axis)


def scatter_blk(parts):
    nb = parts.shape[0]
    parts = parts.reshape((nb // 2, 2) + parts.shape[1:])
    got = swap(parts[:, 1].astype(bf16), "blk", 1)
    mine = parts[:, 0] + got.astype(f32)
    total = mine[0]
    for k in range(1, nb // 2):
        total = total + swap(mine[k].astype(bf16), "blk", 2 * k).astype(f32)
    return total


def normalize(values):
    average = jnp.mean(values, axis=-1, keepdims=True)
    centred = values - average
    inverse = lax.rsqrt(jnp.mean(centred * centred, axis=-1, keepdims=True) + 1e-06)
    return (centred * inverse, inverse)


def normalize_back(grad_normed, normed, inverse):
    return inverse * (
        grad_normed
        - jnp.mean(grad_normed, axis=-1, keepdims=True)
        - normed * jnp.mean(grad_normed * normed, axis=-1, keepdims=True)
    )


def contract(left, right, left_dim, right_dim):
    return lax.dot_general(
        left, right, (((left_dim,), (right_dim,)), ((), ())), preferred_element_type=f32
    )


def precise(left, right, left_dim=1, right_dim=0):
    return lax.dot_general(
        left,
        right,
        (((left_dim,), (right_dim,)), ((), ())),
        precision=lax.Precision.HIGHEST,
        preferred_element_type=f32,
    )


def gelu_both(values):
    scale = math.sqrt(2.0 / math.pi)
    square = values * values
    inner = jnp.tanh(values * (scale + (scale * 0.044715) * square))
    half = 0.5 + 0.5 * inner
    slope = half + (0.5 * values) * (1.0 - inner * inner) * (
        scale + (3.0 * scale * 0.044715) * square
    )
    return values * half, slope


def expert_pass(rows, grads, up, down, sums):
    hidden, slope = gelu_both(contract(rows, up[...], 1, 0))
    hidden = hidden.astype(bf16)
    grad_pre = (contract(grads, down[...], 1, 0) * slope).astype(bf16)
    sums[0] += contract(rows, grad_pre, 0, 0)
    sums[1] += contract(grads, hidden, 0, 0)
    return contract(hidden, down[...], 1, 1), contract(grad_pre, up[...], 1, 1)


def pieces_of(values):
    high = values.astype(bf16)
    rest = values - high.astype(f32)
    middle = rest.astype(bf16)
    return high, middle, (rest - middle.astype(f32)).astype(bf16)


def coded(values, mask, experts):
    kind = lax.broadcasted_iota(jnp.int32, (1, LANES), 1) // experts
    high, middle, low = (p.astype(f32) for p in pieces_of(values))
    return jnp.where(
        mask, jnp.where(kind == 0, high, jnp.where(kind == 1, middle, low)), 0.0
    ).astype(bf16)


class Stream:
    def __init__(self, weights, buffer, sems, keep, send, keep_buffer, send_buffer, out_sems):
        self.weights, self.buffer, self.sems = weights, buffer, sems
        self.outs = ((keep_buffer, keep), (send_buffer, send))
        self.out_sems = out_sems

    def copies(self, at):
        slot, half = at % 2, self.buffer.shape[3] // 2
        return [
            pltpu.make_async_copy(
                ref, self.buffer.at[slot, :, :, i * half : (i + 1) * half], self.sems.at[slot, i]
            )
            for i, ref in enumerate(self.weights(at))
        ]

    def start(self, at):
        for copy in self.copies(at):
            copy.start()

    def wait(self, at):
        for copy in self.copies(at):
            copy.wait()

    def out_copies(self, at):
        return [
            pltpu.make_async_copy(buffer, ref.at[at], self.out_sems.at[i])
            for i, (buffer, ref) in enumerate(self.outs)
        ]

    def put(self, at, sums):
        if at > 0:
            self.finish(at - 1)
        half = sums.shape[2] // 2
        self.outs[0][0][...] = sums[:, :, :half]
        self.outs[1][0][...] = sums[:, :, half:].astype(bf16)
        for copy in self.out_copies(at):
            copy.start()

    def finish(self, at):
        for copy in self.out_copies(at):
            copy.wait()


def stream_scratch(width):
    half = width // 2
    return [
        pltpu.VMEM((2, 2, D, width), bf16),
        pltpu.VMEM((2, D, half), f32),
        pltpu.VMEM((2, D, half), bf16),
        pltpu.SemaphoreType.DMA((2, 2)),
        pltpu.SemaphoreType.DMA((2,)),
    ]


def shared_rows(tokens_ref, grads_ref, buffer, sums, total_ref, first):
    count = tokens_ref.shape[0]
    step_rows = min(count, 2 * ROWS)

    def one(step, carry):
        at = pl.ds(pl.multiple_of(step * step_rows, step_rows), step_rows)
        forward, backward = expert_pass(
            tokens_ref[at, :D], grads_ref[at], buffer.at[0], buffer.at[1], sums
        )
        if first:
            total_ref[at, :D] = forward
            total_ref[at, D : 2 * D] = backward
        else:
            total_ref[at, :D] += forward
            total_ref[at, D : 2 * D] += backward
        return carry

    lax.fori_loop(0, count // step_rows, one, 0)


def shared_first_kernel(
    tokens_ref, grads_ref, own_ref, other_ref, total_ref, sums_ref, buffer, sems
):
    members = own_ref.shape[0]
    stream = Stream(
        lambda m: (own_ref.at[m], other_ref.at[m]), buffer, sems, None, None, None, None, None
    )
    stream.start(0)
    total_ref[:, 2 * D :] = jnp.zeros((total_ref.shape[0], LANES), f32)
    for m in range(members):
        if m + 1 < members:
            stream.start(m + 1)
        stream.wait(m)
        sums = sums_ref.at[m]
        sums[...] = jnp.zeros(sums.shape, f32)
        shared_rows(tokens_ref, grads_ref, buffer.at[m % 2], sums, total_ref, m == 0)


def shared_second_kernel(
    tokens_ref,
    grads_ref,
    own_ref,
    other_ref,
    before_ref,
    total_ref,
    keep_ref,
    send_ref,
    buffer,
    keep_buffer,
    send_buffer,
    sems,
    out_sems,
    sums,
):
    members = own_ref.shape[0]
    stream = Stream(
        lambda m: (own_ref.at[m], other_ref.at[m]),
        buffer,
        sems,
        keep_ref,
        send_ref,
        keep_buffer,
        send_buffer,
        out_sems,
    )
    stream.start(0)
    total_ref[:, 2 * D :] = jnp.zeros((total_ref.shape[0], LANES), f32)
    for m in range(members):
        if m + 1 < members:
            stream.start(m + 1)
        stream.wait(m)
        sums[...] = before_ref[m]
        shared_rows(tokens_ref, grads_ref, buffer.at[m % 2], sums, total_ref, m == 0)
        stream.put(m, sums)
    stream.finish(members - 1)


IN_VMEM = pl.BlockSpec(memory_space=pltpu.VMEM)
ANYWHERE = pl.BlockSpec(memory_space=pl.ANY)


def ordered(kernel, inputs, gates):
    return lambda *refs: kernel(*refs[:inputs], *refs[inputs + len(gates) :])


def cost(us, bytes_accessed=0):
    return pl.CostEstimate(
        flops=int(us * COST_UNIT), bytes_accessed=bytes_accessed, transcendentals=0
    )


def shared_first_call(tokens, own, other, gates=()):
    count = tokens[0].shape[0]
    members, _, _, half = own.shape
    return pl.pallas_call(
        ordered(shared_first_kernel, 4, gates),
        in_specs=[IN_VMEM, IN_VMEM, ANYWHERE, ANYWHERE] + [ANYWHERE] * len(gates),
        out_specs=[IN_VMEM, IN_VMEM],
        out_shape=[
            jax.ShapeDtypeStruct((count, WIDE), f32),
            jax.ShapeDtypeStruct((members, 2, D, 2 * half), f32),
        ],
        scratch_shapes=[
            pltpu.VMEM((2, 2, D, 2 * half), bf16),
            pltpu.SemaphoreType.DMA((2, 2)),
        ],
        compiler_params=pltpu.CompilerParams(vmem_limit_bytes=EXPERT_VMEM),
        cost_estimate=cost(13.0),
        name="shared_experts_own",
    )(*tokens, own, other, *gates)


def shared_second_call(tokens, own, other, sums, gates=()):
    count = tokens[0].shape[0]
    members, _, _, half = own.shape
    return pl.pallas_call(
        ordered(shared_second_kernel, 5, gates),
        in_specs=[IN_VMEM, IN_VMEM, ANYWHERE, ANYWHERE, IN_VMEM] + [ANYWHERE] * len(gates),
        out_specs=[IN_VMEM, ANYWHERE, ANYWHERE],
        out_shape=[
            jax.ShapeDtypeStruct((count, WIDE), f32),
            jax.ShapeDtypeStruct((members, 2, D, half), f32),
            jax.ShapeDtypeStruct((members, 2, D, half), bf16),
        ],
        scratch_shapes=stream_scratch(2 * half) + [pltpu.VMEM((2, D, 2 * half), f32)],
        compiler_params=pltpu.CompilerParams(vmem_limit_bytes=EXPERT_VMEM),
        cost_estimate=cost(15.0),
        name="shared_experts_partner",
    )(*tokens, own, other, sums, *gates)


def routed_kernel(*refs, batch, experts):
    table_ref = refs[0]
    tokens, grads_in, slots = refs[1:3], refs[3:5], refs[5:7]
    weights = refs[7 : 7 + 2 * batch]
    totals = refs[9 + 2 * batch : 11 + 2 * batch]
    keep_ref, send_ref = refs[11 + 2 * batch : 13 + 2 * batch]
    buffer, keep_buffer, send_buffer, sems, out_sems, sums = refs[13 + 2 * batch :]
    stream = Stream(
        lambda e: weights[2 * e : 2 * e + 2],
        buffer,
        sems,
        keep_ref,
        send_ref,
        keep_buffer,
        send_buffer,
        out_sems,
    )
    stream.start(0)
    lane = lax.broadcasted_iota(jnp.int32, (1, LANES), 1)
    for e in range(batch):
        if e + 1 < batch:
            stream.start(e + 1)
        stream.wait(e)
        sums[...] = jnp.zeros(sums.shape, f32)
        expert = table_ref[e, 4]
        mine = (lane % experts == expert) & (lane < 3 * experts)
        for part in range(2):
            first = table_ref[e, 2 * part]
            steps = (table_ref[e, 2 * part + 1] * BLOCK + ROWS - 1) // ROWS

            def one(step, carry):
                places = slots[part][pl.ds(expert, 1), :] - (first * BLOCK + step * ROWS)
                hits = places == lax.broadcasted_iota(jnp.int32, (ROWS, 1), 0)
                hits = jnp.where(hits, 1.0, 0.0).astype(bf16)
                taken = contract(hits, tokens[part][...], 1, 0)
                grad_moe = contract(hits, grads_in[part][...], 1, 0)
                gate = jnp.sum(jnp.where(mine, taken[:, D:], 0.0), axis=1, keepdims=True)
                forward, backward = expert_pass(
                    taken[:, :D].astype(bf16),
                    (gate * grad_moe).astype(bf16),
                    buffer.at[e % 2, 0],
                    buffer.at[e % 2, 1],
                    sums,
                )
                dots = jnp.sum(grad_moe * forward, axis=1, keepdims=True)
                spread = jnp.concatenate(
                    [
                        (gate * forward).astype(bf16),
                        backward.astype(bf16),
                        coded(dots, mine, experts),
                    ],
                    axis=1,
                )
                totals[part][...] += contract(hits, spread, 0, 0)
                return carry

            lax.fori_loop(0, steps, one, 0)
        stream.put(e, sums)
    stream.finish(batch - 1)


def routed_call(table, tokens, grads, slots, weights, totals, gates=()):
    count = tokens[0].shape[0]
    experts = slots[0].shape[0]
    batch = table.shape[0]
    half = weights[0].shape[2]
    at = 7 + 2 * batch
    return pl.pallas_call(
        ordered(
            functools.partial(routed_kernel, batch=batch, experts=experts), 9 + 2 * batch, gates
        ),
        in_specs=[pl.BlockSpec(memory_space=pltpu.SMEM)]
        + [IN_VMEM] * 6
        + [ANYWHERE] * (2 * batch)
        + [IN_VMEM] * 2
        + [ANYWHERE] * len(gates),
        out_specs=[IN_VMEM, IN_VMEM, ANYWHERE, ANYWHERE],
        out_shape=[
            jax.ShapeDtypeStruct((count, WIDE), f32),
            jax.ShapeDtypeStruct((count, WIDE), f32),
            jax.ShapeDtypeStruct((batch, 2, D, half), f32),
            jax.ShapeDtypeStruct((batch, 2, D, half), bf16),
        ],
        scratch_shapes=stream_scratch(2 * half) + [pltpu.VMEM((2, D, 2 * half), f32)],
        input_output_aliases={at: 0, at + 1: 1},
        compiler_params=pltpu.CompilerParams(vmem_limit_bytes=EXPERT_VMEM),
        cost_estimate=cost(11.5 * batch),
        name="routed_experts",
    )(table, *tokens, *grads, *slots, *weights, *totals, *gates)


def attention_kernel(
    tokens_ref,
    mod_ref,
    qkv_ref,
    out_ref,
    router_ref,
    ids_ref,
    slots_ref,
    moment_ref,
    cond_ref,
    packed_ref,
    mixed_ref,
    middle_ref,
    tokens_out_ref,
    gates_ref,
    places_ref,
    moment_out_ref,
    cond_out_ref,
):
    moment_out_ref[...] = moment_ref[...]
    cond_out_ref[...] = cond_ref[...]
    values_in = tokens_ref[...].astype(f32)
    mod = mod_ref[0]
    normed, _ = normalize(values_in)
    attn_in = (normed * (1.0 + mod[1:2]) + mod[0:1]).astype(bf16)
    packed = contract(attn_in, qkv_ref[...], 1, 0).astype(bf16)
    packed_ref[...] = packed
    mixed = []
    for head in range(HEADS):
        queries, keys, values = (
            packed[:, base + head * HD : base + (head + 1) * HD] for base in (0, D, 2 * D)
        )
        scores = contract(queries, keys, 1, 1) * HD ** (-0.5)
        expo = jnp.exp(scores - jnp.max(scores, axis=-1, keepdims=True))
        prob = (expo / jnp.sum(expo, axis=-1, keepdims=True)).astype(bf16)
        mixed.append(contract(prob, values, 1, 0).astype(bf16))
    mixed = jnp.concatenate(mixed, axis=1)
    mixed_ref[...] = mixed
    middle = values_in + mod[2:3] * contract(mixed, out_ref[...], 1, 0)
    middle_ref[...] = middle
    normed, _ = normalize(middle)
    moe_in = (normed * (1.0 + mod[4:5]) + mod[3:4]).astype(bf16)
    tokens_out_ref[:, :D] = moe_in
    logits = contract(moe_in, router_ref[...], 1, 0)
    experts = lax.broadcasted_iota(jnp.int32, logits.shape, 1)
    chosen = [
        jnp.sum(jnp.where(ids_ref[:, j : j + 1] == experts, logits, 0.0), axis=1, keepdims=True)
        for j in range(2)
    ]
    top = jnp.maximum(chosen[0], chosen[1])
    weight = [jnp.exp(c - top) for c in chosen]
    both = weight[0] + weight[1]
    gates = [weight[0] / both, weight[1] / both]
    gates_ref[...] = jnp.concatenate(gates, axis=1)
    count = router_ref.shape[1]
    lane = lax.broadcasted_iota(jnp.int32, (1, LANES), 1)
    lane = jnp.where(lane < 3 * count, lane % count, -1)
    coded_gates = jnp.zeros((SEQ, LANES), f32)
    for j in range(2):
        coded_gates = jnp.where(ids_ref[:, j : j + 1] == lane, gates[j], coded_gates)
    tokens_out_ref[:, D:] = coded(coded_gates, lane >= 0, count)
    lane = lax.broadcasted_iota(jnp.int32, (1, LANES), 1)
    places = jnp.where(
        ids_ref[:, 0:1] == lane,
        slots_ref[:, 0:1],
        jnp.where(ids_ref[:, 1:2] == lane, slots_ref[:, 1:2], -1),
    )
    places_ref[...] = jnp.transpose(places.astype(f32))[:count].astype(jnp.int32)


def image_rows(width):
    return pl.BlockSpec((SEQ, width), lambda n: (n, 0))


def whole(*shape):
    return pl.BlockSpec(shape, lambda n: (0,) * len(shape))


def attention_call(tokens, mod, qkv, out, router, ids, slots, moment, cond, gates=()):
    count, experts = tokens.shape[0], router.shape[1]
    images = count // SEQ
    return pl.pallas_call(
        ordered(attention_kernel, 9, gates),
        grid=(images,),
        in_specs=[
            image_rows(D),
            pl.BlockSpec((1, 6, D), lambda n: (n, 0, 0)),
            whole(D, 3 * D),
            whole(D, D),
            whole(D, experts),
            image_rows(2),
            image_rows(2),
            whole(*moment.shape),
            whole(*cond.shape),
        ]
        + [ANYWHERE] * len(gates),
        out_specs=[
            image_rows(3 * D),
            image_rows(D),
            image_rows(D),
            image_rows(D + LANES),
            image_rows(2),
            pl.BlockSpec((experts, SEQ), lambda n: (0, n)),
            whole(*moment.shape),
            whole(*cond.shape),
        ],
        out_shape=[
            jax.ShapeDtypeStruct((count, 3 * D), bf16),
            jax.ShapeDtypeStruct((count, D), bf16),
            jax.ShapeDtypeStruct((count, D), f32),
            jax.ShapeDtypeStruct((count, D + LANES), bf16),
            jax.ShapeDtypeStruct((count, 2), f32),
            jax.ShapeDtypeStruct((experts, count), jnp.int32),
            jax.ShapeDtypeStruct(moment.shape, f32),
            jax.ShapeDtypeStruct(cond.shape, bf16),
        ],
        compiler_params=pltpu.CompilerParams(vmem_limit_bytes=VMEM_LIMIT),
        cost_estimate=cost(14.0),
        name="attention_forward",
    )(tokens, mod, qkv, out, router, ids, slots, moment, cond, *gates)


def attention_back_kernel(
    me_ref,
    tokens_ref,
    mod_ref,
    qkv_ref,
    out_ref,
    router_ref,
    ids_ref,
    packed_ref,
    mixed_ref,
    middle_ref,
    tokens_two_ref,
    gates_ref,
    total_ref,
    other_ref,
    grad_ref,
    block_out_ref,
    grad_tokens_ref,
    grad_mod_ref,
    small_ref,
    grad_qkv_ref,
    grad_out_ref,
    grad_router_ref,
):
    mod = mod_ref[0]
    grad = grad_ref[...].astype(f32)
    total = total_ref[...] + other_ref[...].astype(f32)
    moe = total[:, :D]
    middle = middle_ref[...]
    block_out_ref[...] = (middle + mod[5:6] * moe).astype(bf16)
    grad_gate_moe = jnp.sum(grad * moe, axis=0, keepdims=True)
    gates = gates_ref[...]
    lane = lax.broadcasted_iota(jnp.int32, (1, LANES), 1)
    lane = jnp.where(lane < 3 * router_ref.shape[1], lane % router_ref.shape[1], -1)
    dots = [
        jnp.sum(
            jnp.where(ids_ref[:, j : j + 1] == lane, total[:, 2 * D :], 0.0), axis=1, keepdims=True
        )
        for j in range(2)
    ]
    blended = gates[:, 0:1] * dots[0] + gates[:, 1:2] * dots[1]
    experts = lax.broadcasted_iota(jnp.int32, (SEQ, router_ref.shape[1]), 1)
    grad_logits = jnp.zeros((SEQ, router_ref.shape[1]), f32)
    for j in range(2):
        grad_chosen = gates[:, j : j + 1] * (dots[j] - blended)
        grad_logits += jnp.where(ids_ref[:, j : j + 1] == experts, grad_chosen, 0.0)
    grad_logits = grad_logits.astype(bf16)
    grad_in = total[:, D : 2 * D] + contract(grad_logits, router_ref[...], 1, 1)
    grad_router = contract(tokens_two_ref[:, :D], grad_logits, 0, 0)
    normed, inverse = normalize(middle)
    grad_shift_moe = jnp.sum(grad_in, axis=0, keepdims=True)
    grad_scale_moe = jnp.sum(grad_in * normed, axis=0, keepdims=True)
    grad_middle = grad + normalize_back(grad_in * (1.0 + mod[4:5]), normed, inverse)
    mixed = mixed_ref[...]
    branch = contract(mixed, out_ref[...], 1, 0)
    grad_gate_attn = jnp.sum(grad_middle * branch, axis=0, keepdims=True)
    grad_branch = (mod[2:3] * grad_middle).astype(bf16)
    grad_out = contract(mixed, grad_branch, 0, 0)
    grad_mixed = contract(grad_branch, out_ref[...], 1, 1).astype(bf16)
    packed = packed_ref[...]
    grads = [[], [], []]
    for head in range(HEADS):
        queries, keys, values = (
            packed[:, base + head * HD : base + (head + 1) * HD] for base in (0, D, 2 * D)
        )
        grad_head = grad_mixed[:, head * HD : (head + 1) * HD]
        scores = contract(queries, keys, 1, 1) * HD ** (-0.5)
        expo = jnp.exp(scores - jnp.max(scores, axis=-1, keepdims=True))
        prob = expo / jnp.sum(expo, axis=-1, keepdims=True)
        grad_prob = contract(grad_head, values, 1, 1)
        delta = jnp.sum(prob * grad_prob, axis=-1, keepdims=True)
        grad_scores = (prob * (grad_prob - delta)).astype(bf16)
        grads[0].append((contract(grad_scores, keys, 1, 0) * HD ** (-0.5)).astype(bf16))
        grads[1].append((contract(grad_scores, queries, 0, 0) * HD ** (-0.5)).astype(bf16))
        grads[2].append(contract(prob.astype(bf16), grad_head, 0, 0).astype(bf16))
    grad_packed = jnp.concatenate(grads[0] + grads[1] + grads[2], axis=1)
    normed, inverse = normalize(tokens_ref[...].astype(f32))
    attn_in = (normed * (1.0 + mod[1:2]) + mod[0:1]).astype(bf16)
    grad_qkv = contract(attn_in, grad_packed, 0, 0)
    grad_in = contract(grad_packed, qkv_ref[...], 1, 1)
    grad_shift = jnp.sum(grad_in, axis=0, keepdims=True)
    grad_scale = jnp.sum(grad_in * normed, axis=0, keepdims=True)
    grad_tokens_ref[...] = grad_middle + normalize_back(
        grad_in * (1.0 + mod[1:2]), normed, inverse
    )
    grad_mod_ref[0] = jnp.concatenate(
        [grad_shift, grad_scale, grad_gate_attn, grad_shift_moe, grad_scale_moe, grad_gate_moe],
        axis=0,
    )

    @pl.when(pl.program_id(0) == 0)
    def _():
        grad_qkv_ref[...] = grad_qkv
        grad_out_ref[...] = grad_out
        grad_router_ref[...] = grad_router

    @pl.when(pl.program_id(0) != 0)
    def _():
        grad_qkv_ref[...] += grad_qkv
        grad_out_ref[...] += grad_out
        grad_router_ref[...] += grad_router

    @pl.when(pl.program_id(0) == pl.num_programs(0) - 1)
    def _():
        columns = small_ref.shape[0]
        for j in range(columns):
            offset = me_ref[0] ^ j
            small_ref[(offset >> 1) + (offset & 1) * (columns // 2)] = jnp.concatenate(
                [
                    ref[:, j * width : (j + 1) * width]
                    for ref, width in (
                        (r, r.shape[1] // columns)
                        for r in (grad_qkv_ref, grad_out_ref, grad_router_ref)
                    )
                ],
                axis=1,
            )


def attention_back_call(
    me, columns, tokens, mod, qkv, out, router, ids, packed, mixed, middle, tokens_two, gates, total, other, grad,
    gates_on=(),
):
    count, experts = tokens.shape[0], router.shape[1]
    images = count // SEQ
    mod_spec = pl.BlockSpec((1, 6, D), lambda n: (n, 0, 0))
    return pl.pallas_call(
        ordered(attention_back_kernel, 15, gates_on),
        grid=(images,),
        in_specs=[
            pl.BlockSpec(memory_space=pltpu.SMEM),
            image_rows(D),
            mod_spec,
            whole(D, 3 * D),
            whole(D, D),
            whole(D, experts),
            image_rows(2),
            image_rows(3 * D),
            image_rows(D),
            image_rows(D),
            image_rows(D + LANES),
            image_rows(2),
            image_rows(WIDE),
            image_rows(WIDE),
            image_rows(D),
        ]
        + [ANYWHERE] * len(gates_on),
        out_specs=[
            image_rows(D),
            image_rows(D),
            mod_spec,
            whole(columns, D, (4 * D + experts) // columns),
        ],
        out_shape=[
            jax.ShapeDtypeStruct((count, D), bf16),
            jax.ShapeDtypeStruct((count, D), f32),
            jax.ShapeDtypeStruct((images, 6, D), f32),
            jax.ShapeDtypeStruct((columns, D, (4 * D + experts) // columns), f32),
        ],
        scratch_shapes=[
            pltpu.VMEM((D, 3 * D), f32),
            pltpu.VMEM((D, D), f32),
            pltpu.VMEM((D, experts), f32),
        ],
        compiler_params=pltpu.CompilerParams(vmem_limit_bytes=VMEM_LIMIT),
        cost_estimate=cost(28.0),
        name="attention_backward",
    )(me, tokens, mod, qkv, out, router, ids, packed, mixed, middle, tokens_two, gates, total, other, grad, *gates_on)


def pack_kernel(*refs):
    refs[-1][...] = jnp.concatenate([ref[...] for ref in refs[:-1]], axis=1).astype(bf16)


def pack_call(weights):
    rows = weights[0].shape[0]
    return pl.pallas_call(
        pack_kernel,
        out_shape=jax.ShapeDtypeStruct((rows, sum(w.shape[1] for w in weights)), bf16),
        cost_estimate=cost(2.0),
        name="pack_small",
    )(*weights)


def round_kernel(up_ref, down_ref, shared_up_ref, shared_down_ref, own_ref, shared_ref):
    own_ref[0] = up_ref[0].astype(bf16)
    own_ref[1] = down_ref[0].astype(bf16)
    for m in range(SHARED):
        shared_ref[m, 0] = shared_up_ref[m].astype(bf16)
        shared_ref[m, 1] = shared_down_ref[m].astype(bf16)


def round_call(up, down, shared_up, shared_down, gates):
    rows, width = shared_up.shape[1:]
    return pl.pallas_call(
        ordered(round_kernel, 4, gates),
        in_specs=[IN_VMEM] * 4 + [ANYWHERE] * len(gates),
        out_shape=[
            jax.ShapeDtypeStruct((2, D, width), bf16),
            jax.ShapeDtypeStruct((SHARED, 2, rows, width), bf16),
        ],
        cost_estimate=cost(3.0),
        name="round_experts",
    )(up, down, shared_up, shared_down, *gates)


def arrange_kernel(me_ref, even_ref, odd_ref, out_ref):
    rows = even_ref.shape[2]
    for odd, ref in enumerate((even_ref, odd_ref)):
        for i in range(ref.shape[0]):
            at = pl.multiple_of((me_ref[0] ^ (2 * i + odd)) * rows, 8)
            out_ref[:, pl.ds(at, rows), :] = ref[i]


def arrange_call(me, even, odd):
    count, stack, rows, width = even.shape
    return pl.pallas_call(
        arrange_kernel,
        in_specs=[pl.BlockSpec(memory_space=pltpu.SMEM), IN_VMEM, IN_VMEM],
        out_shape=jax.ShapeDtypeStruct((stack, 2 * count * rows, width), even.dtype),
        compiler_params=pltpu.CompilerParams(vmem_limit_bytes=VMEM_LIMIT),
        cost_estimate=cost(3.0),
        name="arrange_rows",
    )(me, even, odd)


def modulation_kernel(
    me_ref, cond_ref, vectors_ref, moment_ref, grad_ref, gram_ref, columns_ref
):
    columns, _, width = moment_ref.shape
    rows = grad_ref.shape[0]
    cond = cond_ref[...]
    cond = jnp.concatenate([cond] * 3, axis=0)
    gram = None
    for j in range(columns):
        vectors = pieces_of(vectors_ref[:, j * width : (j + 1) * width])
        grad = contract(cond, jnp.concatenate(vectors, axis=0), 0, 0)
        new = 0.5 * moment_ref[j] + grad
        high, middle, low = pieces_of(new)
        for left, right in ((high, high), (middle, middle)):
            term = contract(left, right, 1, 1)
            gram = term if gram is None else gram + term
        for left, right in ((high, middle), (high, low)):
            term = contract(left, right, 1, 1)
            gram = gram + term + term.T

        @pl.when(me_ref[1] == j)
        def _():
            columns_ref[...] = new
            grad_ref[...] = grad

    gram_ref[...] = gram


def modulation_call(me, cond, vectors, moment):
    _, rows, width = moment.shape
    return pl.pallas_call(
        modulation_kernel,
        in_specs=[pl.BlockSpec(memory_space=pltpu.SMEM)] + [IN_VMEM] * 3,
        out_shape=[
            jax.ShapeDtypeStruct((rows, width), f32),
            jax.ShapeDtypeStruct((rows, rows), f32),
            jax.ShapeDtypeStruct((rows, width), f32),
        ],
        compiler_params=pltpu.CompilerParams(vmem_limit_bytes=2 * VMEM_LIMIT),
        cost_estimate=cost(8.0),
        name="modulation_update",
    )(me, cond, vectors, moment)


def assemble_kernel(*refs, layout, cuts):
    me_ref, cond_ref, grad_ref = refs[:3]
    pieces = refs[3 : 3 + len(layout)]
    full_refs = refs[3 + len(layout) : 7 + len(layout)]
    mod_ref, grads_ref, buffer, sem = refs[7 + len(layout) :]
    rows = pieces[0].shape[1]
    copies = []
    for ref, (odd, column, start) in zip(pieces, layout, strict=True):
        for i in range(ref.shape[0]):
            at = (me_ref[0] ^ (2 * (start + i) + odd)) * rows
            copies.append(
                pltpu.make_async_copy(
                    ref.at[i],
                    buffer.at[me_ref[1] ^ column, pl.ds(pl.multiple_of(at, 16), rows), :],
                    sem.at[len(copies)],
                )
            )
    for copy in copies:
        copy.start()
    for copy in copies:
        copy.wait()
    for ref, start, end in zip(full_refs, cuts[:-1], cuts[1:], strict=True):
        ref[...] = jnp.concatenate(
            [buffer[j, :, start:end] for j in range(buffer.shape[0])], axis=1
        )
    mod = contract(cond_ref[...], full_refs[0][...], 1, 0)
    for i in range(6):
        mod_ref[:, i, :] = mod[:, i * D : (i + 1) * D]
    for n in range(mod.shape[0]):
        at = slice(n * SEQ, (n + 1) * SEQ)
        grads_ref[at] = (mod[n : n + 1, 5 * D :] * grad_ref[at].astype(f32)).astype(bf16)


def assemble_call(me, cond, grad, pieces, layout, cuts, columns):
    images, count = cond.shape[0], grad.shape[0]
    return pl.pallas_call(
        functools.partial(assemble_kernel, layout=layout, cuts=cuts),
        in_specs=[pl.BlockSpec(memory_space=pltpu.SMEM), IN_VMEM, IN_VMEM]
        + [ANYWHERE] * len(pieces),
        out_shape=[
            jax.ShapeDtypeStruct((D, columns * (end - start)), bf16)
            for start, end in zip(cuts[:-1], cuts[1:], strict=True)
        ]
        + [
            jax.ShapeDtypeStruct((images, 6, D), f32),
            jax.ShapeDtypeStruct((count, D), bf16),
        ],
        scratch_shapes=[
            pltpu.VMEM((columns, D, cuts[-1]), bf16),
            pltpu.SemaphoreType.DMA((sum(p.shape[0] for p in pieces),)),
        ],
        compiler_params=pltpu.CompilerParams(vmem_limit_bytes=VMEM_LIMIT),
        cost_estimate=cost(5.0),
        name="assemble_small",
    )(me, cond, grad, *pieces)


def product(left, right, parts):
    left, right = pieces_of(left), pieces_of(right)
    terms = ((0, 0), (0, 1), (1, 0), (0, 2), (2, 0), (1, 1))[: 6 if parts == 3 else 3]
    return contract(
        jnp.concatenate([left[i] for i, _ in terms], axis=1),
        jnp.concatenate([right[j] for _, j in terms], axis=0),
        1,
        0,
    )


def polish_kernel(gram_ref, mixer_ref):
    count, size, _ = gram_ref.shape
    identity = lax.broadcasted_iota(jnp.int32, (size, size), 0) == lax.broadcasted_iota(
        jnp.int32, (size, size), 1
    )
    state = []
    for i in range(count):
        gram = gram_ref[i]
        squares = jnp.sum(jnp.where(identity, gram, 0.0), axis=(0, 1), keepdims=True)
        scale = 1.0 / (jnp.sqrt(squares) + 1e-07)
        state.append((gram * (scale * scale), None, scale))
    for step in range(NS_STEPS):
        parts = 3 if step < 2 else 2
        after_step = []
        for gram, mixer, scale in state:
            poly = cubic_term * gram + quintic_term * product(gram, gram, parts)
            poly = jnp.where(identity, linear_term + poly, poly)
            if step == NS_STEPS - 1:
                mixer = product(poly, mixer, parts)
            elif step == 0:
                mixer, gram = poly, product(poly, product(gram, poly, parts), parts)
            else:
                both = jnp.concatenate([product(gram, poly, parts), mixer], axis=1)
                both = product(poly, both, parts)
                gram, mixer = both[:, :size], both[:, size:]
            after_step.append((gram, mixer, scale))
        state = after_step
    for i in range(count):
        mixer_ref[i] = state[i][1] * state[i][2]


def polish_call(grams, name):
    count, size, _ = grams.shape
    return pl.pallas_call(
        polish_kernel,
        out_shape=jax.ShapeDtypeStruct(grams.shape, f32),
        compiler_params=pltpu.CompilerParams(vmem_limit_bytes=VMEM_LIMIT),
        cost_estimate=cost(13.0 * count if size > 128 else 4.0),
        name=name,
    )(grams)


def stacked_precise(left, right, left_dim, right_dim):
    return lax.dot_general(
        left,
        right,
        (((left_dim,), (right_dim,)), ((0,), (0,))),
        precision=lax.Precision.HIGHEST,
        preferred_element_type=f32,
    )


def on_device(
    tokens_in,
    condition,
    grad_output,
    expert_ids,
    slot_rows,
    expert_counts,
    ada_weight,
    ada_moment,
    qkv_weight,
    qkv_moment,
    out_weight,
    out_moment,
    router_weight,
    router_moment,
    shared_up,
    shared_up_moment,
    shared_down,
    shared_down_moment,
    expert_up,
    expert_up_moment,
    expert_down,
    expert_down_moment,
):
    count = tokens_in.shape[0]
    images = count // SEQ
    nb, nd = lax.axis_size("blk"), lax.axis_size("dp")
    blk, dp = lax.axis_index("blk"), lax.axis_index("dp")
    blk_masks = bits("blk")[1:] + [1]
    dp_masks = bits("dp")
    col_masks = [m for m in dp_masks if m != TP]
    high_masks = [m for m in dp_masks if m not in (1, TP)]
    height = ada_weight.shape[0]
    wide_ada, wide_qkv, wide_out, wide_router = (
        w.shape[1] for w in (ada_weight, qkv_weight, out_weight, router_weight)
    )
    cuts = (0, wide_ada, wide_ada + wide_qkv, wide_ada + wide_qkv + wide_out)

    me = jnp.stack([blk, dp]).astype(jnp.int32)
    half = nb // 4

    def over_z(own):
        return jnp.stack([own] + [swap(own, "blk", 2 * k) for k in range(1, nb // 2)])

    def collect(own):
        even = over_z(own)
        return arrange_call(me, even, swap(even, "blk", 1))

    cond_low = jax.nn.silu(condition).astype(bf16)
    small = over_z(pack_call((ada_weight, qkv_weight, out_weight, router_weight)))
    small_x, small_y = swap(small, "blk", 1), swap(small, "dp", TP)
    pieces = [
        (small, 0, 0, 0),
        (small_x, 1, 0, 0),
        (small_y, 0, TP, 0),
        (swap(small_y[:half], "blk", 1), 1, TP, 0),
        (swap(small_x[half:], "dp", TP), 1, TP, half),
    ]
    for mask in high_masks + [1]:
        pieces = pieces + [
            (swap(piece, "dp", mask), odd, column ^ mask, start)
            for piece, odd, column, start in pieces
        ]
    ada_full, qkv_full, out_full, router_full, modulation, grad_moe = assemble_call(
        me,
        cond_low,
        grad_output,
        [p[0] for p in pieces],
        [p[1:] for p in pieces],
        cuts + (cuts[-1] + wide_router,),
        nd,
    )

    def other_half(own):
        for mask in high_masks[::-1]:
            own = jnp.concatenate([own, swap(own, "dp", mask)], axis=-1)
        return own, swap(own, "dp", 1)

    expert_own, shared_rows_own = round_call(
        expert_up, expert_down, shared_up, shared_down, (small_x, small_y)
    )
    shared = collect(shared_rows_own.reshape((2 * SHARED,) + shared_rows_own.shape[2:]))
    shared = shared.reshape(SHARED, 2, D, -1)
    shared_own, shared_other = other_half(shared)

    pairs = []
    for k in range(nb // 2):
        first = expert_own if k == 0 else swap(expert_own, "blk", 2 * k)
        pairs.append(other_half(first) + other_half(swap(first, "blk", 1)))

    def everywhere(rows):
        rows = over_z(rows)
        rows_x, rows_y = swap(rows, "blk", 1), swap(rows, "dp", TP)
        rows = jnp.concatenate(
            [rows, rows_x, rows_y, swap(rows_y[:half], "blk", 1), swap(rows_x[half:], "dp", TP)]
        )
        for mask in high_masks + [1]:
            rows = jnp.concatenate([rows, swap(rows, "dp", mask)])
        return rows.reshape(-1, rows.shape[-1])

    block_count = (expert_counts[0] + BLOCK - 1) // BLOCK
    block_first = jnp.cumsum(block_count) - block_count
    blocks = jnp.stack([block_first, block_count], axis=1)
    blocks = jnp.concatenate([blocks, swap(blocks, "dp", TP)], axis=1)

    partner_grads = swap(grad_moe, "dp", TP)
    packed, mixed, middle, tokens_two, gates, places, ada_moment_later, cond_later = attention_call(
        tokens_in,
        modulation,
        qkv_full,
        out_full,
        router_full,
        expert_ids,
        slot_rows,
        ada_moment,
        cond_low,
        gates=(pairs[1][0],),
    )
    places = (places, swap(places, "dp", TP))
    tokens_pair = (tokens_two, swap(tokens_two, "dp", TP))
    grads_pair = (grad_moe, partner_grads)

    def merge(keep, send):
        grads = keep + swap(send, "dp", 1).astype(f32)
        for mask in high_masks:
            half = grads.shape[-1] // 2
            got = swap(grads[..., half:].astype(bf16), "dp", mask)
            grads = grads[..., :half] + got.astype(f32)
        return grads

    def over_x(grads):
        return grads[0] + swap(grads[1].astype(bf16), "blk", 1).astype(f32)

    total, sums = shared_first_call(
        (tokens_pair[0], grads_pair[0]), shared_own, shared_other, gates=(pairs[2][0], pairs[0][3])
    )
    total_two, keep, send = shared_second_call(
        (tokens_pair[1], grads_pair[1]), shared_own, shared_other, sums, gates=(pairs[3][0],)
    )
    totals = (total, total_two)
    merged = [merge(keep, send)]

    def shared_piece(offset):
        at = (blk ^ offset) * height
        return lax.dynamic_slice_in_dim(merged[0], at, height, 2)

    odd = jnp.stack([shared_piece(j) for j in range(1, nb, 2)])
    even = jnp.stack([shared_piece(j) for j in range(0, nb, 2)])
    halved = [over_x((even, odd))]
    shared_sum = halved[0][0]
    for k in range(1, nb // 2):
        shared_sum = shared_sum + swap(halved[0][k].astype(bf16), "blk", 2 * k).astype(f32)
    shared_up_grad, shared_down_grad = shared_sum[:, 0], shared_sum[:, 1]

    for k in range(nb // 2):
        table = []
        for r in (2 * k, 2 * k + 1):
            line = lax.dynamic_index_in_dim(blocks, blk ^ r, 0, False)
            table.append(jnp.concatenate([line, (blk ^ r)[None]]))
        waits = merged[-2:-1] + halved[-1:] if k > 1 else merged[:k]
        if k > 1:
            halved.append(over_x(merged[k - 1]))
            waits = [merged[k - 1]] + [halved[k - 2]]
        total, total_two, keep, send = routed_call(
            jnp.stack(table), tokens_pair, grads_pair, places, pairs[k], totals, gates=waits
        )
        totals = (total, total_two)
        merged.append(merge(keep, send))
    for grads in merged[len(halved) :]:
        halved.append(over_x(grads))
    expert_grads = halved[1]
    for k in range(1, nb // 2):
        expert_grads = expert_grads + swap(halved[k + 1].astype(bf16), "blk", 2 * k).astype(f32)

    other = swap(totals[1].astype(bf16), "dp", TP)

    cond_all = everywhere(cond_later)
    ada_moment_full = collect(ada_moment_later[None])
    offsets = [0]
    for mask in dp_masks[::-1]:
        ada_moment_full = jnp.concatenate([ada_moment_full, swap(ada_moment_full, "dp", mask)])
        offsets = offsets + [o ^ mask for o in offsets]
    ada_moment_full = in_order(ada_moment_full, offsets, "dp")

    block_out, grad_tokens, grad_mod, small_grads = attention_back_call(
        me[1:],
        nd,
        tokens_in,
        modulation,
        qkv_full,
        out_full,
        router_full,
        expert_ids,
        packed,
        mixed,
        middle,
        tokens_two,
        gates,
        totals[0],
        other,
        grad_output,
        gates_on=(halved[-1],),
    )
    grad_mod = grad_mod.reshape(images, 6 * D)
    grad_silu = precise(grad_mod, ada_full.astype(f32), 1, 1)
    grad_condition = jax.vjp(jax.nn.silu, condition)[1](grad_silu)[0]

    for mask in [1] + [m for m in dp_masks[::-1] if m != 1]:
        part = small_grads.shape[0] // 2
        got = swap(small_grads[part:].astype(bf16), "dp", mask)
        small_grads = small_grads[:part] + got.astype(f32)
    small_grads = scatter_blk(by_offset(small_grads[0].reshape(nb, height, -1), "blk"))
    small_cuts = (0, wide_qkv, wide_qkv + wide_out)
    qkv_grad = small_grads[:, : small_cuts[1]]
    out_grad = small_grads[:, small_cuts[1] : small_cuts[2]]
    router_grad = small_grads[:, small_cuts[2] :]

    vectors = everywhere(grad_mod)
    ada_grad_cols, ada_gram, ada_cols = modulation_call(me, cond_all, vectors, ada_moment_full)

    def own_block(matrix, width):
        return lax.dynamic_slice(matrix, (blk * height, dp * width), (height, width))

    def own_rows(stack):
        return lax.dynamic_slice_in_dim(stack, blk * height, height, stack.ndim - 2)

    ada_grad = own_rows(ada_grad_cols)

    expert_up_grad, expert_down_grad = expert_grads[0:1], expert_grads[1:2]
    ada_moment_new = 0.5 * ada_moment + ada_grad
    qkv_moment_new = 0.5 * qkv_moment + qkv_grad
    out_moment_new = 0.5 * out_moment + out_grad
    router_moment_new = 0.5 * router_moment + router_grad
    shared_up_moment_new = 0.5 * shared_up_moment + shared_up_grad
    shared_down_moment_new = 0.5 * shared_down_moment + shared_down_grad
    expert_up_moment_new = 0.5 * expert_up_moment + expert_up_grad
    expert_down_moment_new = 0.5 * expert_down_moment + expert_down_grad

    core = dp & 1

    def halve(stack):
        half = stack.shape[0] // 2
        mine = jnp.where(core == 0, stack[:half], stack[half:])
        theirs = jnp.where(core == 0, stack[half:], stack[:half])
        return mine + swap(theirs, "dp", 1)

    def join(mine):
        theirs = swap(mine, "dp", 1)
        return jnp.concatenate(
            [jnp.where(core == 0, mine, theirs), jnp.where(core == 0, theirs, mine)]
        )

    expert_new = jnp.concatenate([expert_up_moment_new, expert_down_moment_new])
    gram = halve(stacked_precise(expert_new, expert_new, 2, 2))
    for mask in [TP] + high_masks:
        gram = gram + swap(gram, "dp", mask)
    orth_expert = stacked_precise(join(polish_call(gram, "polish_experts")), expert_new, 2, 1)

    shared_new = jnp.concatenate([shared_up_moment_new, shared_down_moment_new])
    shared_cols = collect(shared_new)
    gram = halve(stacked_precise(shared_cols, shared_cols, 2, 2))
    upper = (dp & TP) != 0
    mine = jnp.where(upper, gram[1:], gram[:1])
    gram = mine + swap(jnp.where(upper, gram[:1], gram[1:]), "dp", TP)
    for mask in high_masks:
        gram = gram + swap(gram, "dp", mask)
    mine = polish_call(gram, "polish_shared")
    theirs = swap(mine, "dp", TP)
    mixer = join(jnp.concatenate([jnp.where(upper, theirs, mine), jnp.where(upper, mine, theirs)]))
    orth_shared = stacked_precise(own_rows(mixer), shared_cols, 2, 1)
    orth_shared_up, orth_shared_down = orth_shared[:SHARED], orth_shared[SHARED:]

    small_new = jnp.concatenate([qkv_moment_new, out_moment_new, router_moment_new], axis=1)
    small_cols = collect(small_new[None])[0]
    qkv_cols = small_cols[:, : small_cuts[1]]
    out_cols = small_cols[:, small_cuts[1] : small_cuts[2]]
    router_cols, offsets = double(small_cols[:, small_cuts[2] :].T, "dp", dp_masks)
    router_whole = in_order(router_cols, offsets, "dp").reshape(-1, D)
    gram = halve(jnp.stack([precise(qkv_cols, qkv_cols, 1, 1), precise(out_cols, out_cols, 1, 1)]))
    for mask in [TP] + high_masks:
        gram = gram + swap(gram, "dp", mask)
    mixer = polish_call(jnp.concatenate([gram, ada_gram[None]]), "polish_dense")
    ada_mixer = mixer[1]
    mixer = join(mixer[0:1])
    orth_ada = precise(own_rows(ada_mixer), ada_cols)
    orth_qkv = precise(own_rows(mixer[0]), qkv_cols)
    orth_out = precise(own_rows(mixer[1]), out_cols)
    experts = router_whole.shape[0]
    router_gram = jnp.pad(
        precise(router_whole, router_whole, 1, 1), ((0, 128 - experts), (0, 128 - experts))
    )
    router_mixer = polish_call(router_gram[None], "polish_router")[0, :experts, :experts]
    orth_router = own_block(precise(router_whole, router_mixer, 0, 1), wide_router)

    ada_new = ada_weight - math.sqrt(6.0) * orth_ada
    qkv_new = qkv_weight - math.sqrt(3.0) * orth_qkv
    out_new = out_weight - math.sqrt(D / (D // 64)) * orth_out
    router_new = router_weight - 0.5 * orth_router
    shared_up_new = shared_up - math.sqrt(FF / D) * orth_shared_up
    shared_down_new = shared_down - 1.0 * orth_shared_down
    expert_up_new = expert_up - math.sqrt(FF / D) * orth_expert[0:1]
    expert_down_new = expert_down - 1.0 * orth_expert[1:2]
    return (
        block_out,
        grad_tokens,
        grad_condition,
        ada_grad,
        ada_moment_new,
        ada_new,
        ada_new.astype(bf16),
        qkv_grad,
        qkv_moment_new,
        qkv_new,
        qkv_new.astype(bf16),
        out_grad,
        out_moment_new,
        out_new,
        out_new.astype(bf16),
        router_grad,
        router_moment_new,
        router_new,
        router_new.astype(bf16),
        shared_up_grad,
        shared_up_moment_new,
        shared_up_new,
        shared_up_new.astype(bf16),
        shared_down_grad,
        shared_down_moment_new,
        shared_down_new,
        shared_down_new.astype(bf16),
        expert_up_grad,
        expert_up_moment_new,
        expert_up_new,
        expert_up_new.astype(bf16),
        expert_down_grad,
        expert_down_moment_new,
        expert_down_new,
        expert_down_new.astype(bf16),
    )


def solution(mesh):
    tokens = P(("blk", "dp"), None)
    dense = P("blk", "dp")
    shared = P(None, "blk", "dp")
    routed = P("blk", None, "dp")
    in_specs = (tokens,) * 6 + (dense,) * 8 + (shared,) * 4 + (routed,) * 4
    out_specs = (tokens,) * 3 + (dense,) * 16 + (shared,) * 8 + (routed,) * 8
    return jax.shard_map(
        on_device, mesh=mesh, in_specs=in_specs, out_specs=out_specs, check_vma=False
    )
```

```python
import functools
import math

import jax
import jax.numpy as jnp
from jax import lax
from jax.experimental import pallas as pl
from jax.experimental.pallas import tpu as pltpu
from jax.sharding import PartitionSpec as P

D = 384
HEADS = 6
HD = 64
FF = 1536
SHARED = 2
SEQ = 256
BLOCK = 128
NS_STEPS = 5
ROWS = 256
TP = 2

linear_term = 3.4445
cubic_term = -4.775
quintic_term = 2.0315

bf16 = jnp.bfloat16
f32 = jnp.float32
VMEM_LIMIT = 24 * 1024 * 1024
EXPERT_VMEM = 32 * 1024 * 1024
LANES = 128
WIDE = 2 * D + LANES
COST_UNIT = 1.2e9


def swap(values, axis, mask):
    count = lax.axis_size(axis)
    return lax.ppermute(values, axis, [(i, i ^ mask) for i in range(count)])


def bits(axis):
    count = lax.axis_size(axis)
    return [1 << i for i in range(count.bit_length() - 1)]


def double(values, axis, masks):
    offsets = [0]
    values = values[None]
    for mask in masks:
        values = jnp.concatenate([values, swap(values, axis, mask)], axis=0)
        offsets = offsets + [o ^ mask for o in offsets]
    return values, offsets


def in_order(values, offsets, axis):
    me = lax.axis_index(axis)
    values = jnp.stack([values[offsets.index(j)] for j in range(len(offsets))])
    for mask in bits(axis):
        flipped = jnp.stack([values[j ^ mask] for j in range(len(offsets))])
        values = jnp.where((me & mask) != 0, flipped, values)
    return values


def by_offset(values, axis):
    return in_order(values, list(range(values.shape[0])), axis)


def scatter_blk(parts):
    nb = parts.shape[0]
    parts = parts.reshape((nb // 2, 2) + parts.shape[1:])
    got = swap(parts[:, 1].astype(bf16), "blk", 1)
    mine = parts[:, 0] + got.astype(f32)
    total = mine[0]
    for k in range(1, nb // 2):
        total = total + swap(mine[k].astype(bf16), "blk", 2 * k).astype(f32)
    return total


def normalize(values):
    average = jnp.mean(values, axis=-1, keepdims=True)
    centred = values - average
    inverse = lax.rsqrt(jnp.mean(centred * centred, axis=-1, keepdims=True) + 1e-06)
    return (centred * inverse, inverse)


def normalize_back(grad_normed, normed, inverse):
    return inverse * (
        grad_normed
        - jnp.mean(grad_normed, axis=-1, keepdims=True)
        - normed * jnp.mean(grad_normed * normed, axis=-1, keepdims=True)
    )


def contract(left, right, left_dim, right_dim):
    return lax.dot_general(
        left, right, (((left_dim,), (right_dim,)), ((), ())), preferred_element_type=f32
    )


def precise(left, right, left_dim=1, right_dim=0):
    return lax.dot_general(
        left,
        right,
        (((left_dim,), (right_dim,)), ((), ())),
        precision=lax.Precision.HIGHEST,
        preferred_element_type=f32,
    )


def gelu_both(values):
    scale = math.sqrt(2.0 / math.pi)
    square = values * values
    inner = jnp.tanh(values * (scale + (scale * 0.044715) * square))
    half = 0.5 + 0.5 * inner
    slope = half + (0.5 * values) * (1.0 - inner * inner) * (
        scale + (3.0 * scale * 0.044715) * square
    )
    return values * half, slope


def expert_pass(rows, grads, up, down, sums):
    hidden, slope = gelu_both(contract(rows, up[...], 1, 0))
    hidden = hidden.astype(bf16)
    grad_pre = (contract(grads, down[...], 1, 0) * slope).astype(bf16)
    sums[0] += contract(rows, grad_pre, 0, 0)
    sums[1] += contract(grads, hidden, 0, 0)
    return contract(hidden, down[...], 1, 1), contract(grad_pre, up[...], 1, 1)


def pieces_of(values):
    high = values.astype(bf16)
    rest = values - high.astype(f32)
    middle = rest.astype(bf16)
    return high, middle, (rest - middle.astype(f32)).astype(bf16)


def coded(values, mask, experts):
    kind = lax.broadcasted_iota(jnp.int32, (1, LANES), 1) // experts
    high, middle, low = (p.astype(f32) for p in pieces_of(values))
    return jnp.where(
        mask, jnp.where(kind == 0, high, jnp.where(kind == 1, middle, low)), 0.0
    ).astype(bf16)


class Stream:
    def __init__(self, weights, buffer, sems, keep, send, keep_buffer, send_buffer, out_sems):
        self.weights, self.buffer, self.sems = weights, buffer, sems
        self.outs = ((keep_buffer, keep), (send_buffer, send))
        self.out_sems = out_sems

    def copies(self, at):
        slot, half = at % 2, self.buffer.shape[3] // 2
        return [
            pltpu.make_async_copy(
                ref, self.buffer.at[slot, :, :, i * half : (i + 1) * half], self.sems.at[slot, i]
            )
            for i, ref in enumerate(self.weights(at))
        ]

    def start(self, at):
        for copy in self.copies(at):
            copy.start()

    def wait(self, at):
        for copy in self.copies(at):
            copy.wait()

    def out_copies(self, at):
        return [
            pltpu.make_async_copy(buffer, ref.at[at], self.out_sems.at[i])
            for i, (buffer, ref) in enumerate(self.outs)
        ]

    def put(self, at, sums):
        if at > 0:
            self.finish(at - 1)
        half = sums.shape[2] // 2
        self.outs[0][0][...] = sums[:, :, :half]
        self.outs[1][0][...] = sums[:, :, half:].astype(bf16)
        for copy in self.out_copies(at):
            copy.start()

    def finish(self, at):
        for copy in self.out_copies(at):
            copy.wait()


def stream_scratch(width):
    half = width // 2
    return [
        pltpu.VMEM((2, 2, D, width), bf16),
        pltpu.VMEM((2, D, half), f32),
        pltpu.VMEM((2, D, half), bf16),
        pltpu.SemaphoreType.DMA((2, 2)),
        pltpu.SemaphoreType.DMA((2,)),
    ]


def shared_rows(tokens_ref, grads_ref, buffer, sums, total_ref, first):
    count = tokens_ref.shape[0]
    step_rows = min(count, 2 * ROWS)

    def one(step, carry):
        at = pl.ds(pl.multiple_of(step * step_rows, step_rows), step_rows)
        forward, backward = expert_pass(
            tokens_ref[at, :D], grads_ref[at], buffer.at[0], buffer.at[1], sums
        )
        if first:
            total_ref[at, :D] = forward
            total_ref[at, D : 2 * D] = backward
        else:
            total_ref[at, :D] += forward
            total_ref[at, D : 2 * D] += backward
        return carry

    lax.fori_loop(0, count // step_rows, one, 0)


class Moves:
    def __init__(self, sems):
        self.sems, self.used = sems, 0

    def start(self, source, target):
        copy = pltpu.make_async_copy(source, target, self.sems.at[self.used])
        self.used += 1
        copy.start()
        return copy


def shared_first_kernel(
    tokens_in, grads_in, own_ref, other_ref, total_out, sums_out,
    buffer, sems, tokens_ref, grads_ref, total_ref, sums, move_sems,
):
    members = own_ref.shape[0]
    moves = Moves(move_sems)
    loads = [moves.start(tokens_in, tokens_ref), moves.start(grads_in, grads_ref)]
    stream = Stream(
        lambda m: (own_ref.at[m], other_ref.at[m]), buffer, sems, None, None, None, None, None
    )
    stream.start(0)
    total_ref[:, 2 * D :] = jnp.zeros((total_ref.shape[0], LANES), f32)
    for copy in loads:
        copy.wait()
    stores = []
    for m in range(members):
        if m + 1 < members:
            stream.start(m + 1)
        stream.wait(m)
        sums[m] = jnp.zeros(sums.shape[1:], f32)
        shared_rows(tokens_ref, grads_ref, buffer.at[m % 2], sums.at[m], total_ref, m == 0)
        stores.append(moves.start(sums.at[m], sums_out.at[m]))
    stores.append(moves.start(total_ref, total_out))
    for copy in stores:
        copy.wait()


def shared_second_kernel(
    tokens_in, grads_in, own_ref, other_ref, before_ref, total_in, total_out, keep_ref, send_ref,
    buffer, keep_buffer, send_buffer, sems, out_sems, tokens_ref, grads_ref, total_ref, sums, move_sems,
):
    members = own_ref.shape[0]
    moves = Moves(move_sems)
    loads = [
        moves.start(tokens_in, tokens_ref),
        moves.start(grads_in, grads_ref),
        moves.start(total_in, total_ref),
    ]
    stream = Stream(
        lambda m: (own_ref.at[m], other_ref.at[m]),
        buffer, sems, keep_ref, send_ref, keep_buffer, send_buffer, out_sems,
    )
    stream.start(0)
    before = [moves.start(before_ref.at[m], sums.at[m]) for m in range(members)]
    for copy in loads:
        copy.wait()
    for m in range(members):
        if m + 1 < members:
            stream.start(m + 1)
        stream.wait(m)
        before[m].wait()
        shared_rows(tokens_ref, grads_ref, buffer.at[m % 2], sums.at[m], total_ref, False)
        stream.put(m, sums.at[m])
    store = moves.start(total_ref, total_out)
    stream.finish(members - 1)
    store.wait()


IN_VMEM = pl.BlockSpec(memory_space=pltpu.VMEM)
ANYWHERE = pl.BlockSpec(memory_space=pl.ANY)
IN_HBM = pl.BlockSpec(memory_space=pltpu.HBM)


def ordered(kernel, inputs, gates):
    return lambda *refs: kernel(*refs[:inputs], *refs[inputs + len(gates) :])


def cost(us, bytes_accessed=0):
    return pl.CostEstimate(
        flops=int(us * COST_UNIT), bytes_accessed=bytes_accessed, transcendentals=0
    )


def shared_scratch(count, members, width):
    return [
        pltpu.VMEM((count, D + LANES), bf16),
        pltpu.VMEM((count, D), bf16),
        pltpu.VMEM((count, WIDE), f32),
        pltpu.VMEM((members, 2, D, width), f32),
        pltpu.SemaphoreType.DMA((4 + members,)),
    ]


def shared_first_call(tokens, own, other, gates=()):
    count = tokens[0].shape[0]
    members, _, _, half = own.shape
    return pl.pallas_call(
        ordered(shared_first_kernel, 4, gates),
        in_specs=[ANYWHERE] * (4 + len(gates)),
        out_specs=[IN_HBM, IN_HBM],
        out_shape=[
            jax.ShapeDtypeStruct((count, WIDE), f32),
            jax.ShapeDtypeStruct((members, 2, D, 2 * half), f32),
        ],
        scratch_shapes=[
            pltpu.VMEM((2, 2, D, 2 * half), bf16),
            pltpu.SemaphoreType.DMA((2, 2)),
        ]
        + shared_scratch(count, members, 2 * half),
        compiler_params=pltpu.CompilerParams(vmem_limit_bytes=EXPERT_VMEM),
        cost_estimate=cost(13.0),
        name="shared_experts_own",
    )(*tokens, own, other, *gates)


def shared_second_call(tokens, own, other, sums, total, gates=()):
    count = tokens[0].shape[0]
    members, _, _, half = own.shape
    return pl.pallas_call(
        ordered(shared_second_kernel, 6, gates),
        in_specs=[ANYWHERE] * 4 + [IN_HBM] * 2 + [ANYWHERE] * len(gates),
        out_specs=[IN_HBM, ANYWHERE, ANYWHERE],
        out_shape=[
            jax.ShapeDtypeStruct((count, WIDE), f32),
            jax.ShapeDtypeStruct((members, 2, D, half), f32),
            jax.ShapeDtypeStruct((members, 2, D, half), bf16),
        ],
        scratch_shapes=stream_scratch(2 * half) + shared_scratch(count, members, 2 * half),
        compiler_params=pltpu.CompilerParams(vmem_limit_bytes=EXPERT_VMEM),
        cost_estimate=cost(15.0),
        name="shared_experts_partner",
    )(*tokens, own, other, sums, total, *gates)


def routed_kernel(*refs, batch, experts):
    table_ref = refs[0]
    tokens_in, grads_in, slots = refs[1:3], refs[3:5], refs[5:7]
    weights = refs[7 : 7 + 2 * batch]
    totals_in = refs[7 + 2 * batch : 9 + 2 * batch]
    totals_out = refs[9 + 2 * batch : 11 + 2 * batch]
    keep_ref, send_ref = refs[11 + 2 * batch : 13 + 2 * batch]
    buffer, keep_buffer, send_buffer, sems, out_sems = refs[13 + 2 * batch : 18 + 2 * batch]
    tokens, grads, totals, sums, move_sems = refs[18 + 2 * batch : 23 + 2 * batch]
    rounded = refs[23 + 2 * batch :]
    stream = Stream(
        lambda e: weights[2 * e : 2 * e + 2],
        buffer,
        sems,
        keep_ref,
        send_ref,
        keep_buffer,
        send_buffer,
        out_sems,
    )
    moves = Moves(move_sems)
    stream.start(0)
    loads = [
        [
            moves.start(tokens_in[p], tokens.at[p]),
            moves.start(grads_in[p], grads.at[p]),
            moves.start(totals_in[p], totals.at[p]),
        ]
        for p in range(2)
    ]
    stores = []
    lane = lax.broadcasted_iota(jnp.int32, (1, LANES), 1)
    for e in range(batch):
        if e + 1 < batch:
            stream.start(e + 1)
        sums[...] = jnp.zeros(sums.shape, f32)
        stream.wait(e)
        expert = table_ref[e, 4]
        mine = (lane % experts == expert) & (lane < 3 * experts)
        for part in range(2):
            if e == 0:
                for copy in loads[part]:
                    copy.wait()
            first = table_ref[e, 2 * part]
            steps = (table_ref[e, 2 * part + 1] * BLOCK + ROWS - 1) // ROWS

            def one(step, carry):
                places = slots[part][pl.ds(expert, 1), :] - (first * BLOCK + step * ROWS)
                hits = places == lax.broadcasted_iota(jnp.int32, (ROWS, 1), 0)
                hits = jnp.where(hits, 1.0, 0.0).astype(bf16)
                taken = contract(hits, tokens[part], 1, 0)
                grad_moe = contract(hits, grads[part], 1, 0)
                gate = jnp.sum(jnp.where(mine, taken[:, D:], 0.0), axis=1, keepdims=True)
                forward, backward = expert_pass(
                    taken[:, :D].astype(bf16),
                    (gate * grad_moe).astype(bf16),
                    buffer.at[e % 2, 0],
                    buffer.at[e % 2, 1],
                    sums,
                )
                dots = jnp.sum(grad_moe * forward, axis=1, keepdims=True)
                spread = jnp.concatenate(
                    [
                        (gate * forward).astype(bf16),
                        backward.astype(bf16),
                        coded(dots, mine, experts),
                    ],
                    axis=1,
                )
                totals[part] += contract(hits, spread, 0, 0)
                return carry

            lax.fori_loop(0, steps, one, 0)
            if e == batch - 1:
                source = totals.at[part]
                if part and rounded:
                    source = rounded[0]
                    source[...] = totals[part].astype(bf16)
                stores.append(moves.start(source, totals_out[part]))
        stream.put(e, sums)
    stream.finish(batch - 1)
    for copy in stores:
        copy.wait()


def routed_call(table, tokens, grads, slots, weights, totals, last, gates=()):
    count = tokens[0].shape[0]
    experts = slots[0].shape[0]
    batch = table.shape[0]
    half = weights[0].shape[2]
    return pl.pallas_call(
        ordered(
            functools.partial(routed_kernel, batch=batch, experts=experts), 9 + 2 * batch, gates
        ),
        in_specs=[pl.BlockSpec(memory_space=pltpu.SMEM)]
        + [ANYWHERE] * 4
        + [IN_VMEM] * 2
        + [ANYWHERE] * (2 * batch)
        + [IN_HBM] * 2
        + [ANYWHERE] * len(gates),
        out_specs=[IN_HBM, ANYWHERE if last else IN_HBM, ANYWHERE, ANYWHERE],
        out_shape=[
            jax.ShapeDtypeStruct((count, WIDE), f32),
            jax.ShapeDtypeStruct((count, WIDE), bf16 if last else f32),
            jax.ShapeDtypeStruct((batch, 2, D, half), f32),
            jax.ShapeDtypeStruct((batch, 2, D, half), bf16),
        ],
        scratch_shapes=stream_scratch(2 * half)
        + [
            pltpu.VMEM((2, count, D + LANES), bf16),
            pltpu.VMEM((2, count, D), bf16),
            pltpu.VMEM((2, count, WIDE), f32),
            pltpu.VMEM((2, D, 2 * half), f32),
            pltpu.SemaphoreType.DMA((8,)),
        ]
        + ([pltpu.VMEM((count, WIDE), bf16)] if last else []),
        compiler_params=pltpu.CompilerParams(vmem_limit_bytes=EXPERT_VMEM),
        cost_estimate=cost(11.5 * batch),
        name="routed_experts",
    )(table, *tokens, *grads, *slots, *weights, *totals, *gates)


def attention_kernel(
    tokens_ref,
    mod_ref,
    qkv_ref,
    out_ref,
    router_ref,
    ids_ref,
    slots_ref,
    packed_ref,
    mixed_ref,
    middle_ref,
    tokens_out_ref,
    gates_ref,
    places_ref,
):
    values_in = tokens_ref[...].astype(f32)
    mod = mod_ref[0]
    normed, _ = normalize(values_in)
    attn_in = (normed * (1.0 + mod[1:2]) + mod[0:1]).astype(bf16)
    packed = contract(attn_in, qkv_ref[...], 1, 0).astype(bf16)
    packed_ref[...] = packed
    mixed = []
    for head in range(HEADS):
        queries, keys, values = (
            packed[:, base + head * HD : base + (head + 1) * HD] for base in (0, D, 2 * D)
        )
        scores = contract(queries, keys, 1, 1) * HD ** (-0.5)
        expo = jnp.exp(scores - jnp.max(scores, axis=-1, keepdims=True))
        prob = (expo / jnp.sum(expo, axis=-1, keepdims=True)).astype(bf16)
        mixed.append(contract(prob, values, 1, 0).astype(bf16))
    mixed = jnp.concatenate(mixed, axis=1)
    mixed_ref[...] = mixed
    middle = values_in + mod[2:3] * contract(mixed, out_ref[...], 1, 0)
    middle_ref[...] = middle
    normed, _ = normalize(middle)
    moe_in = (normed * (1.0 + mod[4:5]) + mod[3:4]).astype(bf16)
    tokens_out_ref[:, :D] = moe_in
    logits = contract(moe_in, router_ref[...], 1, 0)
    experts = lax.broadcasted_iota(jnp.int32, logits.shape, 1)
    chosen = [
        jnp.sum(jnp.where(ids_ref[:, j : j + 1] == experts, logits, 0.0), axis=1, keepdims=True)
        for j in range(2)
    ]
    top = jnp.maximum(chosen[0], chosen[1])
    weight = [jnp.exp(c - top) for c in chosen]
    both = weight[0] + weight[1]
    gates = [weight[0] / both, weight[1] / both]
    gates_ref[...] = jnp.concatenate(gates, axis=1)
    count = router_ref.shape[1]
    lane = lax.broadcasted_iota(jnp.int32, (1, LANES), 1)
    lane = jnp.where(lane < 3 * count, lane % count, -1)
    coded_gates = jnp.zeros((SEQ, LANES), f32)
    for j in range(2):
        coded_gates = jnp.where(ids_ref[:, j : j + 1] == lane, gates[j], coded_gates)
    tokens_out_ref[:, D:] = coded(coded_gates, lane >= 0, count)
    lane = lax.broadcasted_iota(jnp.int32, (1, LANES), 1)
    places = jnp.where(
        ids_ref[:, 0:1] == lane,
        slots_ref[:, 0:1],
        jnp.where(ids_ref[:, 1:2] == lane, slots_ref[:, 1:2], -1),
    )
    places_ref[...] = jnp.transpose(places.astype(f32))[:count].astype(jnp.int32)


def image_rows(width):
    return pl.BlockSpec((SEQ, width), lambda n: (n, 0))


def whole(*shape):
    return pl.BlockSpec(shape, lambda n: (0,) * len(shape))


def attention_call(tokens, mod, qkv, out, router, ids, slots, gates=()):
    count, experts = tokens.shape[0], router.shape[1]
    images = count // SEQ
    return pl.pallas_call(
        ordered(attention_kernel, 7, gates),
        grid=(images,),
        in_specs=[
            image_rows(D),
            pl.BlockSpec((1, 6, D), lambda n: (n, 0, 0)),
            whole(D, 3 * D),
            whole(D, D),
            whole(D, experts),
            image_rows(2),
            image_rows(2),
        ]
        + [ANYWHERE] * len(gates),
        out_specs=[
            image_rows(3 * D),
            image_rows(D),
            image_rows(D),
            image_rows(D + LANES),
            image_rows(2),
            pl.BlockSpec((experts, SEQ), lambda n: (0, n)),
        ],
        out_shape=[
            jax.ShapeDtypeStruct((count, 3 * D), bf16),
            jax.ShapeDtypeStruct((count, D), bf16),
            jax.ShapeDtypeStruct((count, D), f32),
            jax.ShapeDtypeStruct((count, D + LANES), bf16),
            jax.ShapeDtypeStruct((count, 2), f32),
            jax.ShapeDtypeStruct((experts, count), jnp.int32),
        ],
        compiler_params=pltpu.CompilerParams(vmem_limit_bytes=VMEM_LIMIT),
        cost_estimate=cost(14.0),
        name="attention_forward",
    )(tokens, mod, qkv, out, router, ids, slots, *gates)


def attention_back_kernel(
    me_ref,
    tokens_ref,
    mod_ref,
    qkv_ref,
    out_ref,
    router_ref,
    ids_ref,
    packed_ref,
    mixed_ref,
    middle_ref,
    tokens_two_ref,
    gates_ref,
    total_ref,
    other_ref,
    grad_ref,
    block_out_ref,
    grad_tokens_ref,
    grad_mod_ref,
    small_ref,
    small_send_ref,
    grad_qkv_ref,
    grad_out_ref,
    grad_router_ref,
):
    mod = mod_ref[0]
    grad = grad_ref[...].astype(f32)
    total = total_ref[...] + other_ref[...].astype(f32)
    moe = total[:, :D]
    middle = middle_ref[...]
    block_out_ref[...] = (middle + mod[5:6] * moe).astype(bf16)
    grad_gate_moe = jnp.sum(grad * moe, axis=0, keepdims=True)
    gates = gates_ref[...]
    lane = lax.broadcasted_iota(jnp.int32, (1, LANES), 1)
    lane = jnp.where(lane < 3 * router_ref.shape[1], lane % router_ref.shape[1], -1)
    dots = [
        jnp.sum(
            jnp.where(ids_ref[:, j : j + 1] == lane, total[:, 2 * D :], 0.0), axis=1, keepdims=True
        )
        for j in range(2)
    ]
    blended = gates[:, 0:1] * dots[0] + gates[:, 1:2] * dots[1]
    experts = lax.broadcasted_iota(jnp.int32, (SEQ, router_ref.shape[1]), 1)
    grad_logits = jnp.zeros((SEQ, router_ref.shape[1]), f32)
    for j in range(2):
        grad_chosen = gates[:, j : j + 1] * (dots[j] - blended)
        grad_logits += jnp.where(ids_ref[:, j : j + 1] == experts, grad_chosen, 0.0)
    grad_logits = grad_logits.astype(bf16)
    grad_in = total[:, D : 2 * D] + contract(grad_logits, router_ref[...], 1, 1)
    grad_router = contract(tokens_two_ref[:, :D], grad_logits, 0, 0)
    normed, inverse = normalize(middle)
    grad_shift_moe = jnp.sum(grad_in, axis=0, keepdims=True)
    grad_scale_moe = jnp.sum(grad_in * normed, axis=0, keepdims=True)
    grad_middle = grad + normalize_back(grad_in * (1.0 + mod[4:5]), normed, inverse)
    mixed = mixed_ref[...]
    branch = contract(mixed, out_ref[...], 1, 0)
    grad_gate_attn = jnp.sum(grad_middle * branch, axis=0, keepdims=True)
    grad_branch = (mod[2:3] * grad_middle).astype(bf16)
    grad_out = contract(mixed, grad_branch, 0, 0)
    grad_mixed = contract(grad_branch, out_ref[...], 1, 1).astype(bf16)
    packed = packed_ref[...]
    grads = [[], [], []]
    for head in range(HEADS):
        queries, keys, values = (
            packed[:, base + head * HD : base + (head + 1) * HD] for base in (0, D, 2 * D)
        )
        grad_head = grad_mixed[:, head * HD : (head + 1) * HD]
        scores = contract(queries, keys, 1, 1) * HD ** (-0.5)
        expo = jnp.exp(scores - jnp.max(scores, axis=-1, keepdims=True))
        prob = expo / jnp.sum(expo, axis=-1, keepdims=True)
        grad_prob = contract(grad_head, values, 1, 1)
        delta = jnp.sum(prob * grad_prob, axis=-1, keepdims=True)
        grad_scores = (prob * (grad_prob - delta)).astype(bf16)
        grads[0].append((contract(grad_scores, keys, 1, 0) * HD ** (-0.5)).astype(bf16))
        grads[1].append((contract(grad_scores, queries, 0, 0) * HD ** (-0.5)).astype(bf16))
        grads[2].append(contract(prob.astype(bf16), grad_head, 0, 0).astype(bf16))
    grad_packed = jnp.concatenate(grads[0] + grads[1] + grads[2], axis=1)
    normed, inverse = normalize(tokens_ref[...].astype(f32))
    attn_in = (normed * (1.0 + mod[1:2]) + mod[0:1]).astype(bf16)
    grad_qkv = contract(attn_in, grad_packed, 0, 0)
    grad_in = contract(grad_packed, qkv_ref[...], 1, 1)
    grad_shift = jnp.sum(grad_in, axis=0, keepdims=True)
    grad_scale = jnp.sum(grad_in * normed, axis=0, keepdims=True)
    grad_tokens_ref[...] = grad_middle + normalize_back(
        grad_in * (1.0 + mod[1:2]), normed, inverse
    )
    grad_mod_ref[0] = jnp.concatenate(
        [grad_shift, grad_scale, grad_gate_attn, grad_shift_moe, grad_scale_moe, grad_gate_moe],
        axis=0,
    )

    @pl.when(pl.program_id(0) == 0)
    def _():
        grad_qkv_ref[...] = grad_qkv
        grad_out_ref[...] = grad_out
        grad_router_ref[...] = grad_router

    @pl.when(pl.program_id(0) != 0)
    def _():
        grad_qkv_ref[...] += grad_qkv
        grad_out_ref[...] += grad_out
        grad_router_ref[...] += grad_router

    @pl.when(pl.program_id(0) == pl.num_programs(0) - 1)
    def _():
        columns = 2 * small_ref.shape[0]
        for j in range(columns):
            offset = me_ref[0] ^ j
            piece = jnp.concatenate(
                [
                    ref[:, j * width : (j + 1) * width]
                    for ref, width in (
                        (r, r.shape[1] // columns)
                        for r in (grad_qkv_ref, grad_out_ref, grad_router_ref)
                    )
                ],
                axis=1,
            )

            @pl.when((offset & 1) == 0)
            def _():
                small_ref[offset >> 1] = piece

            @pl.when((offset & 1) == 1)
            def _():
                small_send_ref[offset >> 1] = piece.astype(bf16)


def attention_back_call(
    me, columns, tokens, mod, qkv, out, router, ids, packed, mixed, middle, tokens_two, gates, total, other, grad,
    gates_on=(),
):
    count, experts = tokens.shape[0], router.shape[1]
    images = count // SEQ
    mod_spec = pl.BlockSpec((1, 6, D), lambda n: (n, 0, 0))
    return pl.pallas_call(
        ordered(attention_back_kernel, 15, gates_on),
        grid=(images,),
        in_specs=[
            pl.BlockSpec(memory_space=pltpu.SMEM),
            image_rows(D),
            mod_spec,
            whole(D, 3 * D),
            whole(D, D),
            whole(D, experts),
            image_rows(2),
            image_rows(3 * D),
            image_rows(D),
            image_rows(D),
            image_rows(D + LANES),
            image_rows(2),
            image_rows(WIDE),
            image_rows(WIDE),
            image_rows(D),
        ]
        + [ANYWHERE] * len(gates_on),
        out_specs=[
            image_rows(D),
            image_rows(D),
            mod_spec,
            whole(columns // 2, D, (4 * D + experts) // columns),
            whole(columns // 2, D, (4 * D + experts) // columns),
        ],
        out_shape=[
            jax.ShapeDtypeStruct((count, D), bf16),
            jax.ShapeDtypeStruct((count, D), f32),
            jax.ShapeDtypeStruct((images, 6, D), f32),
            jax.ShapeDtypeStruct((columns // 2, D, (4 * D + experts) // columns), f32),
            jax.ShapeDtypeStruct((columns // 2, D, (4 * D + experts) // columns), bf16),
        ],
        scratch_shapes=[
            pltpu.VMEM((D, 3 * D), f32),
            pltpu.VMEM((D, D), f32),
            pltpu.VMEM((D, experts), f32),
        ],
        compiler_params=pltpu.CompilerParams(vmem_limit_bytes=VMEM_LIMIT),
        cost_estimate=cost(28.0),
        name="attention_backward",
    )(me, tokens, mod, qkv, out, router, ids, packed, mixed, middle, tokens_two, gates, total, other, grad, *gates_on)


def pack_kernel(*refs):
    refs[-1][...] = jnp.concatenate([ref[...] for ref in refs[:-1]], axis=1).astype(bf16)


def pack_call(weights):
    rows = weights[0].shape[0]
    return pl.pallas_call(
        pack_kernel,
        out_shape=jax.ShapeDtypeStruct((rows, sum(w.shape[1] for w in weights)), bf16),
        cost_estimate=cost(2.0),
        name="pack_small",
    )(*weights)


def round_kernel(up_ref, down_ref, own_ref):
    for m in range(up_ref.shape[0]):
        own_ref[2 * m] = up_ref[m].astype(bf16)
        own_ref[2 * m + 1] = down_ref[m].astype(bf16)


def round_call(up, down, gates):
    count, rows, width = up.shape
    return pl.pallas_call(
        ordered(round_kernel, 2, gates),
        in_specs=[IN_VMEM] * 2 + [ANYWHERE] * len(gates),
        out_shape=jax.ShapeDtypeStruct((2 * count, rows, width), bf16),
        cost_estimate=cost(1.5),
        name="round_experts",
    )(up, down, *gates)


def gram_of(values):
    high, middle, low = pieces_of(values)
    gram = contract(high, high, 1, 1) + contract(middle, middle, 1, 1)
    for right in (middle, low):
        term = contract(high, right, 1, 1)
        gram = gram + term + term.T
    return gram


def update_kernel(*refs, parts, moments, grams):
    out = refs[parts + moments :]
    for i in range(refs[0].shape[0]):
        grad = refs[0][i].astype(f32)
        for ref in refs[1:parts]:
            grad = grad + ref[i].astype(f32)
        which, at = i % moments, i // moments
        new = 0.5 * refs[parts + which][at] + grad
        out[which][at] = grad
        out[moments + which][at] = new
        if grams:
            out[2 * moments][i] = gram_of(new)


def update_call(parts, moments, gates, grams, name):
    stack = parts[0].shape[0]
    outs = [jax.ShapeDtypeStruct(m.shape, f32) for m in moments] * 2
    if grams:
        outs.append(jax.ShapeDtypeStruct((stack, D, D), f32))
    return pl.pallas_call(
        ordered(
            functools.partial(update_kernel, parts=len(parts), moments=len(moments), grams=grams),
            len(parts) + len(moments),
            gates,
        ),
        in_specs=[IN_VMEM] * (len(parts) + len(moments)) + [ANYWHERE] * len(gates),
        out_shape=outs,
        compiler_params=pltpu.CompilerParams(vmem_limit_bytes=VMEM_LIMIT),
        cost_estimate=cost(4.0 if grams else 2.0),
        name=name,
    )(*parts, *moments, *gates)


def arrange_kernel(me_ref, even_ref, odd_ref, out_ref):
    rows = even_ref.shape[2]
    for odd, ref in enumerate((even_ref, odd_ref)):
        for i in range(ref.shape[0]):
            at = pl.multiple_of((me_ref[0] ^ (2 * i + odd)) * rows, 8)
            out_ref[:, pl.ds(at, rows), :] = ref[i]


def arrange_call(me, even, odd):
    count, stack, rows, width = even.shape
    return pl.pallas_call(
        arrange_kernel,
        in_specs=[pl.BlockSpec(memory_space=pltpu.SMEM), IN_VMEM, IN_VMEM],
        out_shape=jax.ShapeDtypeStruct((stack, 2 * count * rows, width), even.dtype),
        compiler_params=pltpu.CompilerParams(vmem_limit_bytes=VMEM_LIMIT),
        cost_estimate=cost(3.0),
        name="arrange_rows",
    )(me, even, odd)


def modulation_kernel(
    me_ref, vectors_ref, moments_ref, grad_ref, gram_ref, columns_ref, *, columns
):
    width = moments_ref.shape[1]
    cond = vectors_ref[:, columns * width :].astype(bf16)
    cond = jnp.concatenate([cond] * 3, axis=0)
    for j in range(columns):

        @pl.when(me_ref[1] == j)
        def _():
            vectors = pieces_of(vectors_ref[:, j * width : (j + 1) * width])
            grad = contract(cond, jnp.concatenate(vectors, axis=0), 0, 0)
            grad_ref[...] = grad
            columns_ref[...] = 0.5 * moments_ref[...] + grad

    gram_ref[...] = gram_of(columns_ref[...])


def modulation_call(me, vectors, moments, columns):
    width = moments.shape[1]
    return pl.pallas_call(
        functools.partial(modulation_kernel, columns=columns),
        in_specs=[pl.BlockSpec(memory_space=pltpu.SMEM)] + [IN_VMEM] * 2,
        out_shape=[
            jax.ShapeDtypeStruct((D, width), f32),
            jax.ShapeDtypeStruct((D, D), f32),
            jax.ShapeDtypeStruct((D, width), f32),
        ],
        compiler_params=pltpu.CompilerParams(vmem_limit_bytes=2 * VMEM_LIMIT),
        cost_estimate=cost(4.0),
        name="modulation_update",
    )(me, vectors, moments)


def assemble_kernel(*refs, layout, cuts):
    me_ref, cond_ref, grad_ref = refs[:3]
    pieces = refs[3 : 3 + len(layout)]
    full_refs = refs[3 + len(layout) : 7 + len(layout)]
    mod_ref, grads_ref, buffer, sem = refs[7 + len(layout) :]
    rows = pieces[0].shape[1]
    copies = []
    for ref, (odd, column, start) in zip(pieces, layout, strict=True):
        for i in range(ref.shape[0]):
            at = (me_ref[0] ^ (2 * (start + i) + odd)) * rows
            copies.append(
                pltpu.make_async_copy(
                    ref.at[i],
                    buffer.at[me_ref[1] ^ column, pl.ds(pl.multiple_of(at, 16), rows), :],
                    sem.at[len(copies)],
                )
            )
    for copy in copies:
        copy.start()
    for copy in copies:
        copy.wait()
    for ref, start, end in zip(full_refs, cuts[:-1], cuts[1:], strict=True):
        ref[...] = jnp.concatenate(
            [buffer[j, :, start:end] for j in range(buffer.shape[0])], axis=1
        )
    mod = contract(cond_ref[...], full_refs[0][...], 1, 0)
    for i in range(6):
        mod_ref[:, i, :] = mod[:, i * D : (i + 1) * D]
    for n in range(mod.shape[0]):
        at = slice(n * SEQ, (n + 1) * SEQ)
        grads_ref[at] = (mod[n : n + 1, 5 * D :] * grad_ref[at].astype(f32)).astype(bf16)


def assemble_call(me, cond, grad, pieces, layout, cuts, columns):
    images, count = cond.shape[0], grad.shape[0]
    return pl.pallas_call(
        functools.partial(assemble_kernel, layout=layout, cuts=cuts),
        in_specs=[pl.BlockSpec(memory_space=pltpu.SMEM), IN_VMEM, IN_VMEM]
        + [ANYWHERE] * len(pieces),
        out_shape=[
            jax.ShapeDtypeStruct((D, columns * (end - start)), bf16)
            for start, end in zip(cuts[:-1], cuts[1:], strict=True)
        ]
        + [
            jax.ShapeDtypeStruct((images, 6, D), f32),
            jax.ShapeDtypeStruct((count, D), bf16),
        ],
        scratch_shapes=[
            pltpu.VMEM((columns, D, cuts[-1]), bf16),
            pltpu.SemaphoreType.DMA((sum(p.shape[0] for p in pieces),)),
        ],
        compiler_params=pltpu.CompilerParams(vmem_limit_bytes=VMEM_LIMIT),
        cost_estimate=cost(5.0),
        name="assemble_small",
    )(me, cond, grad, *pieces)


def product(left, right, parts):
    left, right = pieces_of(left), pieces_of(right)
    terms = ((0, 0), (0, 1), (1, 0), (0, 2), (2, 0), (1, 1))[: 6 if parts == 3 else 3]
    return contract(
        jnp.concatenate([left[i] for i, _ in terms], axis=1),
        jnp.concatenate([right[j] for _, j in terms], axis=0),
        1,
        0,
    )


def polish_kernel(gram_ref, mixer_ref):
    count, size, _ = gram_ref.shape
    identity = lax.broadcasted_iota(jnp.int32, (size, size), 0) == lax.broadcasted_iota(
        jnp.int32, (size, size), 1
    )
    state = []
    for i in range(count):
        gram = gram_ref[i]
        squares = jnp.sum(jnp.where(identity, gram, 0.0), axis=(0, 1), keepdims=True)
        scale = 1.0 / (jnp.sqrt(squares) + 1e-07)
        state.append((gram * (scale * scale), None, scale))
    for step in range(NS_STEPS):
        parts = 3 if step < 2 else 2
        after_step = []
        for gram, mixer, scale in state:
            poly = cubic_term * gram + quintic_term * product(gram, gram, parts)
            poly = jnp.where(identity, linear_term + poly, poly)
            if step == NS_STEPS - 1:
                mixer = product(poly, mixer, parts)
            elif step == 0:
                mixer, gram = poly, product(poly, product(gram, poly, parts), parts)
            else:
                both = jnp.concatenate([product(gram, poly, parts), mixer], axis=1)
                both = product(poly, both, parts)
                gram, mixer = both[:, :size], both[:, size:]
            after_step.append((gram, mixer, scale))
        state = after_step
    for i in range(count):
        mixer_ref[i] = state[i][1] * state[i][2]


def polish_call(grams, name):
    count, size, _ = grams.shape
    return pl.pallas_call(
        polish_kernel,
        out_shape=jax.ShapeDtypeStruct(grams.shape, f32),
        compiler_params=pltpu.CompilerParams(vmem_limit_bytes=VMEM_LIMIT),
        cost_estimate=cost(13.0 * count if size > 128 else 4.0),
        name=name,
    )(grams)


def stacked_precise(left, right, left_dim, right_dim):
    return lax.dot_general(
        left,
        right,
        (((left_dim,), (right_dim,)), ((0,), (0,))),
        precision=lax.Precision.HIGHEST,
        preferred_element_type=f32,
    )


def on_device(
    tokens_in,
    condition,
    grad_output,
    expert_ids,
    slot_rows,
    expert_counts,
    ada_weight,
    ada_moment,
    qkv_weight,
    qkv_moment,
    out_weight,
    out_moment,
    router_weight,
    router_moment,
    shared_up,
    shared_up_moment,
    shared_down,
    shared_down_moment,
    expert_up,
    expert_up_moment,
    expert_down,
    expert_down_moment,
):
    count = tokens_in.shape[0]
    images = count // SEQ
    nb, nd = lax.axis_size("blk"), lax.axis_size("dp")
    blk, dp = lax.axis_index("blk"), lax.axis_index("dp")
    blk_masks = bits("blk")[1:] + [1]
    dp_masks = bits("dp")
    col_masks = [m for m in dp_masks if m != TP]
    high_masks = [m for m in dp_masks if m not in (1, TP)]
    height = ada_weight.shape[0]
    wide_ada, wide_qkv, wide_out, wide_router = (
        w.shape[1] for w in (ada_weight, qkv_weight, out_weight, router_weight)
    )
    cuts = (0, wide_ada, wide_ada + wide_qkv, wide_ada + wide_qkv + wide_out)

    me = jnp.stack([blk, dp]).astype(jnp.int32)
    half = nb // 4

    def over_z(own):
        return jnp.stack([own] + [swap(own, "blk", 2 * k) for k in range(1, nb // 2)])

    def collect(own):
        even = over_z(own)
        return arrange_call(me, even, swap(even, "blk", 1))

    cond_low = jax.nn.silu(condition).astype(bf16)
    small = over_z(pack_call((ada_weight, qkv_weight, out_weight, router_weight)))
    small_x, small_y = swap(small, "blk", 1), swap(small, "dp", TP)
    pieces = [
        (small, 0, 0, 0),
        (small_x, 1, 0, 0),
        (small_y, 0, TP, 0),
        (swap(small_y[:half], "blk", 1), 1, TP, 0),
        (swap(small_x[half:], "dp", TP), 1, TP, half),
    ]
    for mask in high_masks + [1]:
        pieces = pieces + [
            (swap(piece, "dp", mask), odd, column ^ mask, start)
            for piece, odd, column, start in pieces
        ]
    ada_full, qkv_full, out_full, router_full, modulation, grad_moe = assemble_call(
        me,
        cond_low,
        grad_output,
        [p[0] for p in pieces],
        [p[1:] for p in pieces],
        cuts + (cuts[-1] + wide_router,),
        nd,
    )

    def other_half(own):
        for mask in high_masks[::-1]:
            own = jnp.concatenate([own, swap(own, "dp", mask)], axis=-1)
        return own, swap(own, "dp", 1)

    shared_even = over_z(round_call(shared_up, shared_down, (pieces[3][0], pieces[4][0])))
    shared = arrange_call(me, shared_even, swap(shared_even, "blk", 1))
    expert_own = round_call(expert_up, expert_down, (shared_even,))
    shared = shared.reshape(SHARED, 2, D, -1)
    shared_own, shared_other = other_half(shared)

    def parent(k):
        return k & (k - 1)

    def over_bit(values, k):
        return swap(values, "blk", 2 * (k & -k))

    firsts = {0: expert_own, 1: over_bit(expert_own, 1)}
    for k in sorted(range(2, nb // 2), key=lambda k: (k.bit_count(), -k)):
        firsts[k] = over_bit(firsts[parent(k)], k)
    pairs = {k: other_half(f) + other_half(swap(f, "blk", 1)) for k, f in firsts.items()}

    def everywhere(rows):
        rows = over_z(rows)
        rows_x, rows_y = swap(rows, "blk", 1), swap(rows, "dp", TP)
        rows = jnp.concatenate(
            [rows, rows_x, rows_y, swap(rows_y[:half], "blk", 1), swap(rows_x[half:], "dp", TP)]
        )
        for mask in high_masks + [1]:
            rows = jnp.concatenate([rows, swap(rows, "dp", mask)])
        return rows.reshape(-1, rows.shape[-1])

    ada_moments = collect(ada_moment[None])[0]

    block_count = (expert_counts[0] + BLOCK - 1) // BLOCK
    block_first = jnp.cumsum(block_count) - block_count
    blocks = jnp.stack([block_first, block_count], axis=1)
    blocks = jnp.concatenate([blocks, swap(blocks, "dp", TP)], axis=1)

    partner_grads = swap(grad_moe, "dp", TP)
    packed, mixed, middle, tokens_two, gates, places = attention_call(
        tokens_in,
        modulation,
        qkv_full,
        out_full,
        router_full,
        expert_ids,
        slot_rows,
    )
    places = (places, swap(places, "dp", TP))
    tokens_pair = (tokens_two, swap(tokens_two, "dp", TP))
    grads_pair = (grad_moe, partner_grads)

    def merge(keep, send):
        grads = keep + swap(send, "dp", 1).astype(f32)
        for mask in high_masks:
            half = grads.shape[-1] // 2
            got = swap(grads[..., half:].astype(bf16), "dp", mask)
            grads = grads[..., :half] + got.astype(f32)
        return grads

    def over_x(grads):
        return grads[0] + swap(grads[1].astype(bf16), "blk", 1).astype(f32)

    def over_x(grads):
        return grads[0] + swap(grads[1].astype(bf16), "blk", 1).astype(f32)

    def from_z(grads, k):
        return swap(grads.astype(bf16), "blk", 2 * k).astype(f32)

    def shared_over_x(grads):
        def piece(offset):
            return lax.dynamic_slice_in_dim(grads, (blk ^ offset) * height, height, 2)

        return over_x([jnp.stack([piece(j) for j in range(o, nb, 2)]) for o in range(2)])

    def routed(k, totals, last=False, gates=()):
        table = []
        for r in (2 * k, 2 * k + 1):
            line = lax.dynamic_index_in_dim(blocks, blk ^ r, 0, False)
            table.append(jnp.concatenate([line, (blk ^ r)[None]]))
        total, total_two, keep, send = routed_call(
            jnp.stack(table), tokens_pair, grads_pair, places, pairs[k], totals, last, gates
        )
        return (total, total_two), merge(keep, send)

    total, sums = shared_first_call(
        (tokens_pair[0], grads_pair[0]), shared_own, shared_other, gates=(partner_grads,)
    )
    order = [1] + list(range(2, nb // 2))[::-1] + [0]
    sums_of = {}

    def halve_x(step):
        k = order[step]
        terms = [merged[step][0], swap(merged[step][1].astype(bf16), "blk", 1)]
        terms = terms + [sums_of[c] for c in range(k + 1, nb // 2) if parent(c) == k]
        if k:
            terms = sum(t.astype(f32) for t in terms)
            sums_of[k] = over_bit(terms.astype(bf16), k)
        return terms

    totals, merged_one = routed(order[0], (total, jnp.zeros(total.shape, f32)))
    total_two, keep, send = shared_second_call(
        (tokens_pair[1], grads_pair[1]), shared_own, shared_other, sums, totals[1]
    )
    totals = (totals[0], total_two)
    merged = [merged_one]
    shared_merged = merge(keep, send)
    for step, k in enumerate(order[1:], 1):
        if step == 1:
            waits = [merged[0]]
        elif step == 2:
            waits = [shared_merged, halve_x(0)[0]]
        else:
            waits = [merged[step - 2]]
            if step == 3:
                shared_halved = shared_over_x(shared_merged)
                waits.append(shared_halved)
            else:
                halve_x(step - 3)
        totals, more = routed(k, totals, step == len(order) - 1, waits)
        merged.append(more)
    for step in range(len(order) - 3, len(order)):
        expert_terms = halve_x(step)
    shared_terms = [shared_halved[0]]
    for k in range(1, nb // 2):
        shared_terms.append(swap(shared_halved[k].astype(bf16), "blk", 2 * k))
    shared_terms = [t.reshape((2 * SHARED,) + t.shape[2:]) for t in shared_terms]
    shared_up_grad, shared_down_grad, shared_up_moment_new, shared_down_moment_new = update_call(
        shared_terms, (shared_up_moment, shared_down_moment), totals[1:], False, "shared_update"
    )

    other = swap(totals[1], "dp", TP)

    block_out, grad_tokens, grad_mod, small_grads, small_send = attention_back_call(
        me[1:],
        nd,
        tokens_in,
        modulation,
        qkv_full,
        out_full,
        router_full,
        expert_ids,
        packed,
        mixed,
        middle,
        tokens_two,
        gates,
        totals[0],
        other,
        grad_output,
        gates_on=(shared_up_grad,),
    )
    grad_mod = grad_mod.reshape(images, 6 * D)
    grad_silu = precise(grad_mod, ada_full.astype(f32), 1, 1)
    grad_condition = jax.vjp(jax.nn.silu, condition)[1](grad_silu)[0]

    small_grads = small_grads + swap(small_send, "dp", 1).astype(f32)
    for mask in [m for m in dp_masks[::-1] if m != 1]:
        part = small_grads.shape[0] // 2
        got = swap(small_grads[part:].astype(bf16), "dp", mask)
        small_grads = small_grads[:part] + got.astype(f32)
    small_grads = scatter_blk(by_offset(small_grads[0].reshape(nb, height, -1), "blk"))
    small_cuts = (0, wide_qkv, wide_qkv + wide_out)
    qkv_grad = small_grads[:, : small_cuts[1]]
    out_grad = small_grads[:, small_cuts[1] : small_cuts[2]]
    router_grad = small_grads[:, small_cuts[2] :]

    vectors = everywhere(jnp.concatenate([grad_mod, cond_low.astype(f32)], axis=1))
    ada_grad_cols, ada_gram, ada_cols = modulation_call(me, vectors, ada_moments, nd)

    def own_block(matrix, width):
        return lax.dynamic_slice(matrix, (blk * height, dp * width), (height, width))

    def own_rows(stack):
        return lax.dynamic_slice_in_dim(stack, blk * height, height, stack.ndim - 2)

    ada_grad = own_rows(ada_grad_cols)

    expert_up_grad, expert_down_grad, expert_up_moment_new, expert_down_moment_new, expert_gram = (
        update_call(
            expert_terms, (expert_up_moment, expert_down_moment), (grad_tokens,), True, "expert_update"
        )
    )
    ada_moment_new = 0.5 * ada_moment + ada_grad
    qkv_moment_new = 0.5 * qkv_moment + qkv_grad
    out_moment_new = 0.5 * out_moment + out_grad
    router_moment_new = 0.5 * router_moment + router_grad

    core = dp & 1

    def halve(stack):
        half = stack.shape[0] // 2
        mine = jnp.where(core == 0, stack[:half], stack[half:])
        theirs = jnp.where(core == 0, stack[half:], stack[:half])
        return mine + swap(theirs, "dp", 1)

    def join(mine):
        theirs = swap(mine, "dp", 1)
        return jnp.concatenate(
            [jnp.where(core == 0, mine, theirs), jnp.where(core == 0, theirs, mine)]
        )

    upper = (dp & TP) != 0

    def solve(gram, name):
        gram = halve(gram)
        mine = jnp.where(upper, gram[1:], gram[:1])
        gram = mine + swap(jnp.where(upper, gram[:1], gram[1:]), "dp", TP)
        for mask in high_masks:
            gram = gram + swap(gram, "dp", mask)
        mine = polish_call(gram, name)
        theirs = swap(mine, "dp", TP)
        return join(
            jnp.concatenate([jnp.where(upper, theirs, mine), jnp.where(upper, mine, theirs)])
        )

    expert_new = jnp.concatenate([expert_up_moment_new, expert_down_moment_new])
    gram = halve(expert_gram)
    for mask in [TP] + high_masks:
        gram = gram + swap(gram, "dp", mask)
    orth_expert = stacked_precise(join(polish_call(gram, "polish_experts")), expert_new, 2, 1)

    shared_new = jnp.concatenate([shared_up_moment_new, shared_down_moment_new])
    shared_cols = jnp.swapaxes(lax.all_gather(shared_new, "blk"), 0, 1)
    shared_cols = shared_cols.reshape(2 * SHARED, D, -1)
    mixer = solve(stacked_precise(shared_cols, shared_cols, 2, 2), "polish_shared")
    orth_shared = stacked_precise(own_rows(mixer), shared_cols, 2, 1)
    orth_shared_up, orth_shared_down = orth_shared[:SHARED], orth_shared[SHARED:]

    small_new = jnp.concatenate([qkv_moment_new, out_moment_new, router_moment_new], axis=1)
    small_cols = collect(small_new[None])[0]
    qkv_cols = small_cols[:, : small_cuts[1]]
    out_cols = small_cols[:, small_cuts[1] : small_cuts[2]]
    router_cols, offsets = double(small_cols[:, small_cuts[2] :].T, "dp", dp_masks)
    router_whole = in_order(router_cols, offsets, "dp").reshape(-1, D)
    gram = [precise(qkv_cols, qkv_cols, 1, 1), precise(out_cols, out_cols, 1, 1), ada_gram]
    mixer = solve(jnp.stack(gram + [jnp.zeros((D, D), f32)]), "polish_dense")
    ada_mixer = mixer[2]
    orth_ada = precise(own_rows(ada_mixer), ada_cols)
    orth_qkv = precise(own_rows(mixer[0]), qkv_cols)
    orth_out = precise(own_rows(mixer[1]), out_cols)
    experts = router_whole.shape[0]
    router_gram = jnp.pad(
        precise(router_whole, router_whole, 1, 1), ((0, 128 - experts), (0, 128 - experts))
    )
    router_mixer = polish_call(router_gram[None], "polish_router")[0, :experts, :experts]
    orth_router = own_block(precise(router_whole, router_mixer, 0, 1), wide_router)

    ada_new = ada_weight - math.sqrt(6.0) * orth_ada
    qkv_new = qkv_weight - math.sqrt(3.0) * orth_qkv
    out_new = out_weight - math.sqrt(D / (D // 64)) * orth_out
    router_new = router_weight - 0.5 * orth_router
    shared_up_new = shared_up - math.sqrt(FF / D) * orth_shared_up
    shared_down_new = shared_down - 1.0 * orth_shared_down
    expert_up_new = expert_up - math.sqrt(FF / D) * orth_expert[0:1]
    expert_down_new = expert_down - 1.0 * orth_expert[1:2]
    return (
        block_out,
        grad_tokens,
        grad_condition,
        ada_grad,
        ada_moment_new,
        ada_new,
        ada_new.astype(bf16),
        qkv_grad,
        qkv_moment_new,
        qkv_new,
        qkv_new.astype(bf16),
        out_grad,
        out_moment_new,
        out_new,
        out_new.astype(bf16),
        router_grad,
        router_moment_new,
        router_new,
        router_new.astype(bf16),
        shared_up_grad,
        shared_up_moment_new,
        shared_up_new,
        shared_up_new.astype(bf16),
        shared_down_grad,
        shared_down_moment_new,
        shared_down_new,
        shared_down_new.astype(bf16),
        expert_up_grad,
        expert_up_moment_new,
        expert_up_new,
        expert_up_new.astype(bf16),
        expert_down_grad,
        expert_down_moment_new,
        expert_down_new,
        expert_down_new.astype(bf16),
    )


def solution(mesh):
    tokens = P(("blk", "dp"), None)
    dense = P("blk", "dp")
    shared = P(None, "blk", "dp")
    routed = P("blk", None, "dp")
    in_specs = (tokens,) * 6 + (dense,) * 8 + (shared,) * 4 + (routed,) * 4
    out_specs = (tokens,) * 3 + (dense,) * 16 + (shared,) * 8 + (routed,) * 8
    return jax.shard_map(
        on_device, mesh=mesh, in_specs=in_specs, out_specs=out_specs, check_vma=False
    )
```

```python
import functools
import math

import jax
import jax.numpy as jnp
from jax import lax
from jax.experimental import pallas as pl
from jax.experimental.pallas import tpu as pltpu
from jax.sharding import PartitionSpec as P

D = 384
HEADS = 6
HD = 64
FF = 1536
SHARED = 2
SEQ = 256
BLOCK = 128
NS_STEPS = 5
ROWS = 256
TP = 2

linear_term = 3.4445
cubic_term = -4.775
quintic_term = 2.0315

bf16 = jnp.bfloat16
f32 = jnp.float32
VMEM_LIMIT = 24 * 1024 * 1024
EXPERT_VMEM = 32 * 1024 * 1024
LANES = 128
WIDE = 2 * D + LANES
COST_UNIT = 1.2e9


def swap(values, axis, mask):
    count = lax.axis_size(axis)
    return lax.ppermute(values, axis, [(i, i ^ mask) for i in range(count)])


def bits(axis):
    count = lax.axis_size(axis)
    return [1 << i for i in range(count.bit_length() - 1)]


def double(values, axis, masks):
    offsets = [0]
    values = values[None]
    for mask in masks:
        values = jnp.concatenate([values, swap(values, axis, mask)], axis=0)
        offsets = offsets + [o ^ mask for o in offsets]
    return values, offsets


def in_order(values, offsets, axis):
    me = lax.axis_index(axis)
    values = jnp.stack([values[offsets.index(j)] for j in range(len(offsets))])
    for mask in bits(axis):
        flipped = jnp.stack([values[j ^ mask] for j in range(len(offsets))])
        values = jnp.where((me & mask) != 0, flipped, values)
    return values


def by_offset(values, axis):
    return in_order(values, list(range(values.shape[0])), axis)


def scatter_blk(parts):
    nb = parts.shape[0]
    parts = parts.reshape((nb // 2, 2) + parts.shape[1:])
    got = swap(parts[:, 1].astype(bf16), "blk", 1)
    mine = parts[:, 0] + got.astype(f32)
    total = mine[0]
    for k in range(1, nb // 2):
        total = total + swap(mine[k].astype(bf16), "blk", 2 * k).astype(f32)
    return total


def normalize(values):
    average = jnp.mean(values, axis=-1, keepdims=True)
    centred = values - average
    inverse = lax.rsqrt(jnp.mean(centred * centred, axis=-1, keepdims=True) + 1e-06)
    return (centred * inverse, inverse)


def normalize_back(grad_normed, normed, inverse):
    return inverse * (
        grad_normed
        - jnp.mean(grad_normed, axis=-1, keepdims=True)
        - normed * jnp.mean(grad_normed * normed, axis=-1, keepdims=True)
    )


def contract(left, right, left_dim, right_dim):
    return lax.dot_general(
        left, right, (((left_dim,), (right_dim,)), ((), ())), preferred_element_type=f32
    )


def precise(left, right, left_dim=1, right_dim=0):
    return lax.dot_general(
        left,
        right,
        (((left_dim,), (right_dim,)), ((), ())),
        precision=lax.Precision.HIGHEST,
        preferred_element_type=f32,
    )


def gelu_both(values):
    scale = math.sqrt(2.0 / math.pi)
    square = values * values
    inner = jnp.tanh(values * (scale + (scale * 0.044715) * square))
    half = 0.5 + 0.5 * inner
    slope = half + (0.5 * values) * (1.0 - inner * inner) * (
        scale + (3.0 * scale * 0.044715) * square
    )
    return values * half, slope


def expert_pass(rows, grads, up, down, sums):
    hidden, slope = gelu_both(contract(rows, up[...], 1, 0))
    hidden = hidden.astype(bf16)
    grad_pre = (contract(grads, down[...], 1, 0) * slope).astype(bf16)
    sums[0] += contract(rows, grad_pre, 0, 0)
    sums[1] += contract(grads, hidden, 0, 0)
    return contract(hidden, down[...], 1, 1), contract(grad_pre, up[...], 1, 1)


def pieces_of(values):
    high = values.astype(bf16)
    rest = values - high.astype(f32)
    middle = rest.astype(bf16)
    return high, middle, (rest - middle.astype(f32)).astype(bf16)


def coded(values, mask, experts):
    kind = lax.broadcasted_iota(jnp.int32, (1, LANES), 1) // experts
    high, middle, low = (p.astype(f32) for p in pieces_of(values))
    return jnp.where(
        mask, jnp.where(kind == 0, high, jnp.where(kind == 1, middle, low)), 0.0
    ).astype(bf16)


class Stream:
    def __init__(self, weights, buffer, sems, keep, send, keep_buffer, send_buffer, out_sems):
        self.weights, self.buffer, self.sems = weights, buffer, sems
        self.outs = ((keep_buffer, keep), (send_buffer, send))
        self.out_sems = out_sems

    def copies(self, at):
        slot, half = at % 2, self.buffer.shape[3] // 2
        return [
            pltpu.make_async_copy(
                ref, self.buffer.at[slot, :, :, i * half : (i + 1) * half], self.sems.at[slot, i]
            )
            for i, ref in enumerate(self.weights(at))
        ]

    def start(self, at):
        for copy in self.copies(at):
            copy.start()

    def wait(self, at):
        for copy in self.copies(at):
            copy.wait()

    def out_copies(self, at):
        return [
            pltpu.make_async_copy(buffer, ref.at[at], self.out_sems.at[i])
            for i, (buffer, ref) in enumerate(self.outs)
        ]

    def put(self, at, sums):
        if at > 0:
            self.finish(at - 1)
        half = sums.shape[2] // 2
        self.outs[0][0][...] = sums[:, :, :half]
        self.outs[1][0][...] = sums[:, :, half:].astype(bf16)
        for copy in self.out_copies(at):
            copy.start()

    def finish(self, at):
        for copy in self.out_copies(at):
            copy.wait()


def stream_scratch(width):
    half = width // 2
    return [
        pltpu.VMEM((2, 2, D, width), bf16),
        pltpu.VMEM((2, D, half), f32),
        pltpu.VMEM((2, D, half), bf16),
        pltpu.SemaphoreType.DMA((2, 2)),
        pltpu.SemaphoreType.DMA((2,)),
    ]


def shared_rows(tokens_ref, grads_ref, buffer, sums, total_ref, first):
    count = tokens_ref.shape[0]
    step_rows = min(count, 2 * ROWS)

    def one(step, carry):
        at = pl.ds(pl.multiple_of(step * step_rows, step_rows), step_rows)
        forward, backward = expert_pass(
            tokens_ref[at, :D], grads_ref[at], buffer.at[0], buffer.at[1], sums
        )
        if first:
            total_ref[at, :D] = forward
            total_ref[at, D : 2 * D] = backward
        else:
            total_ref[at, :D] += forward
            total_ref[at, D : 2 * D] += backward
        return carry

    lax.fori_loop(0, count // step_rows, one, 0)


class Moves:
    def __init__(self, sems):
        self.sems, self.used = sems, 0

    def start(self, source, target):
        copy = pltpu.make_async_copy(source, target, self.sems.at[self.used])
        self.used += 1
        copy.start()
        return copy


def shared_first_kernel(
    tokens_in, grads_in, own_ref, other_ref, total_out, sums_out,
    buffer, sems, tokens_ref, grads_ref, total_ref, sums, move_sems,
):
    members = own_ref.shape[0]
    moves = Moves(move_sems)
    loads = [moves.start(tokens_in, tokens_ref), moves.start(grads_in, grads_ref)]
    stream = Stream(
        lambda m: (own_ref.at[m], other_ref.at[m]), buffer, sems, None, None, None, None, None
    )
    stream.start(0)
    total_ref[:, 2 * D :] = jnp.zeros((total_ref.shape[0], LANES), f32)
    for copy in loads:
        copy.wait()
    stores = []
    for m in range(members):
        if m + 1 < members:
            stream.start(m + 1)
        stream.wait(m)
        sums[m] = jnp.zeros(sums.shape[1:], f32)
        shared_rows(tokens_ref, grads_ref, buffer.at[m % 2], sums.at[m], total_ref, m == 0)
        stores.append(moves.start(sums.at[m], sums_out.at[m]))
    stores.append(moves.start(total_ref, total_out))
    for copy in stores:
        copy.wait()


def shared_second_kernel(
    tokens_in, grads_in, own_ref, other_ref, before_ref, total_in, total_out, keep_ref, send_ref,
    buffer, keep_buffer, send_buffer, sems, out_sems, tokens_ref, grads_ref, total_ref, sums, move_sems,
):
    members = own_ref.shape[0]
    moves = Moves(move_sems)
    loads = [
        moves.start(tokens_in, tokens_ref),
        moves.start(grads_in, grads_ref),
        moves.start(total_in, total_ref),
    ]
    stream = Stream(
        lambda m: (own_ref.at[m], other_ref.at[m]),
        buffer, sems, keep_ref, send_ref, keep_buffer, send_buffer, out_sems,
    )
    stream.start(0)
    before = [moves.start(before_ref.at[m], sums.at[m]) for m in range(members)]
    for copy in loads:
        copy.wait()
    for m in range(members):
        if m + 1 < members:
            stream.start(m + 1)
        stream.wait(m)
        before[m].wait()
        shared_rows(tokens_ref, grads_ref, buffer.at[m % 2], sums.at[m], total_ref, False)
        stream.put(m, sums.at[m])
    store = moves.start(total_ref, total_out)
    stream.finish(members - 1)
    store.wait()


IN_VMEM = pl.BlockSpec(memory_space=pltpu.VMEM)
ANYWHERE = pl.BlockSpec(memory_space=pl.ANY)
IN_HBM = pl.BlockSpec(memory_space=pltpu.HBM)


def ordered(kernel, inputs, gates):
    return lambda *refs: kernel(*refs[:inputs], *refs[inputs + len(gates) :])


def cost(us, bytes_accessed=0):
    return pl.CostEstimate(
        flops=int(us * COST_UNIT), bytes_accessed=bytes_accessed, transcendentals=0
    )


def shared_scratch(count, members, width):
    return [
        pltpu.VMEM((count, D + LANES), bf16),
        pltpu.VMEM((count, D), bf16),
        pltpu.VMEM((count, WIDE), f32),
        pltpu.VMEM((members, 2, D, width), f32),
        pltpu.SemaphoreType.DMA((4 + members,)),
    ]


def shared_first_call(tokens, own, other, gates=()):
    count = tokens[0].shape[0]
    members, _, _, half = own.shape
    return pl.pallas_call(
        ordered(shared_first_kernel, 4, gates),
        in_specs=[ANYWHERE] * (4 + len(gates)),
        out_specs=[IN_HBM, IN_HBM],
        out_shape=[
            jax.ShapeDtypeStruct((count, WIDE), f32),
            jax.ShapeDtypeStruct((members, 2, D, 2 * half), f32),
        ],
        scratch_shapes=[
            pltpu.VMEM((2, 2, D, 2 * half), bf16),
            pltpu.SemaphoreType.DMA((2, 2)),
        ]
        + shared_scratch(count, members, 2 * half),
        compiler_params=pltpu.CompilerParams(vmem_limit_bytes=EXPERT_VMEM),
        cost_estimate=cost(13.0),
        name="shared_experts_own",
    )(*tokens, own, other, *gates)


def shared_second_call(tokens, own, other, sums, total, gates=()):
    count = tokens[0].shape[0]
    members, _, _, half = own.shape
    return pl.pallas_call(
        ordered(shared_second_kernel, 6, gates),
        in_specs=[ANYWHERE] * 4 + [IN_HBM] * 2 + [ANYWHERE] * len(gates),
        out_specs=[IN_HBM, ANYWHERE, ANYWHERE],
        out_shape=[
            jax.ShapeDtypeStruct((count, WIDE), f32),
            jax.ShapeDtypeStruct((members, 2, D, half), f32),
            jax.ShapeDtypeStruct((members, 2, D, half), bf16),
        ],
        scratch_shapes=stream_scratch(2 * half) + shared_scratch(count, members, 2 * half),
        compiler_params=pltpu.CompilerParams(vmem_limit_bytes=EXPERT_VMEM),
        cost_estimate=cost(15.0),
        name="shared_experts_partner",
    )(*tokens, own, other, sums, total, *gates)


def routed_kernel(*refs, batch, experts):
    table_ref = refs[0]
    tokens_in, grads_in, slots = refs[1:3], refs[3:5], refs[5:7]
    weights = refs[7 : 7 + 2 * batch]
    totals_in = refs[7 + 2 * batch : 9 + 2 * batch]
    totals_out = refs[9 + 2 * batch : 11 + 2 * batch]
    keep_ref, send_ref = refs[11 + 2 * batch : 13 + 2 * batch]
    buffer, keep_buffer, send_buffer, sems, out_sems = refs[13 + 2 * batch : 18 + 2 * batch]
    tokens, grads, totals, sums, move_sems = refs[18 + 2 * batch : 23 + 2 * batch]
    rounded = refs[23 + 2 * batch :]
    stream = Stream(
        lambda e: weights[2 * e : 2 * e + 2],
        buffer,
        sems,
        keep_ref,
        send_ref,
        keep_buffer,
        send_buffer,
        out_sems,
    )
    moves = Moves(move_sems)
    stream.start(0)
    loads = [
        [
            moves.start(tokens_in[p], tokens.at[p]),
            moves.start(grads_in[p], grads.at[p]),
            moves.start(totals_in[p], totals.at[p]),
        ]
        for p in range(2)
    ]
    stores = []
    lane = lax.broadcasted_iota(jnp.int32, (1, LANES), 1)
    for e in range(batch):
        if e + 1 < batch:
            stream.start(e + 1)
        sums[...] = jnp.zeros(sums.shape, f32)
        stream.wait(e)
        expert = table_ref[e, 4]
        mine = (lane % experts == expert) & (lane < 3 * experts)
        for part in range(2):
            if e == 0:
                for copy in loads[part]:
                    copy.wait()
            first = table_ref[e, 2 * part]
            steps = (table_ref[e, 2 * part + 1] * BLOCK + ROWS - 1) // ROWS

            def one(step, carry):
                places = slots[part][pl.ds(expert, 1), :] - (first * BLOCK + step * ROWS)
                hits = places == lax.broadcasted_iota(jnp.int32, (ROWS, 1), 0)
                hits = jnp.where(hits, 1.0, 0.0).astype(bf16)
                taken = contract(hits, tokens[part], 1, 0)
                grad_moe = contract(hits, grads[part], 1, 0)
                gate = jnp.sum(jnp.where(mine, taken[:, D:], 0.0), axis=1, keepdims=True)
                forward, backward = expert_pass(
                    taken[:, :D].astype(bf16),
                    (gate * grad_moe).astype(bf16),
                    buffer.at[e % 2, 0],
                    buffer.at[e % 2, 1],
                    sums,
                )
                dots = jnp.sum(grad_moe * forward, axis=1, keepdims=True)
                spread = jnp.concatenate(
                    [
                        (gate * forward).astype(bf16),
                        backward.astype(bf16),
                        coded(dots, mine, experts),
                    ],
                    axis=1,
                )
                totals[part] += contract(hits, spread, 0, 0)
                return carry

            lax.fori_loop(0, steps, one, 0)
            if e == batch - 1:
                source = totals.at[part]
                if part and rounded:
                    source = rounded[0]
                    source[...] = totals[part].astype(bf16)
                stores.append(moves.start(source, totals_out[part]))
        stream.put(e, sums)
    stream.finish(batch - 1)
    for copy in stores:
        copy.wait()


def routed_call(table, tokens, grads, slots, weights, totals, last, gates=()):
    count = tokens[0].shape[0]
    experts = slots[0].shape[0]
    batch = table.shape[0]
    half = weights[0].shape[2]
    return pl.pallas_call(
        ordered(
            functools.partial(routed_kernel, batch=batch, experts=experts), 9 + 2 * batch, gates
        ),
        in_specs=[pl.BlockSpec(memory_space=pltpu.SMEM)]
        + [ANYWHERE] * 4
        + [IN_VMEM] * 2
        + [ANYWHERE] * (2 * batch)
        + [IN_HBM] * 2
        + [ANYWHERE] * len(gates),
        out_specs=[IN_HBM, ANYWHERE if last else IN_HBM, ANYWHERE, ANYWHERE],
        out_shape=[
            jax.ShapeDtypeStruct((count, WIDE), f32),
            jax.ShapeDtypeStruct((count, WIDE), bf16 if last else f32),
            jax.ShapeDtypeStruct((batch, 2, D, half), f32),
            jax.ShapeDtypeStruct((batch, 2, D, half), bf16),
        ],
        scratch_shapes=stream_scratch(2 * half)
        + [
            pltpu.VMEM((2, count, D + LANES), bf16),
            pltpu.VMEM((2, count, D), bf16),
            pltpu.VMEM((2, count, WIDE), f32),
            pltpu.VMEM((2, D, 2 * half), f32),
            pltpu.SemaphoreType.DMA((8,)),
        ]
        + ([pltpu.VMEM((count, WIDE), bf16)] if last else []),
        compiler_params=pltpu.CompilerParams(vmem_limit_bytes=EXPERT_VMEM),
        cost_estimate=cost(11.5 * batch),
        name="routed_experts",
    )(table, *tokens, *grads, *slots, *weights, *totals, *gates)


def attention_kernel(
    tokens_ref,
    mod_ref,
    qkv_ref,
    out_ref,
    router_ref,
    ids_ref,
    slots_ref,
    packed_ref,
    mixed_ref,
    middle_ref,
    tokens_out_ref,
    gates_ref,
    places_ref,
):
    values_in = tokens_ref[...].astype(f32)
    mod = mod_ref[0]
    normed, _ = normalize(values_in)
    attn_in = (normed * (1.0 + mod[1:2]) + mod[0:1]).astype(bf16)
    packed = contract(attn_in, qkv_ref[...], 1, 0).astype(bf16)
    packed_ref[...] = packed
    mixed = []
    for head in range(HEADS):
        queries, keys, values = (
            packed[:, base + head * HD : base + (head + 1) * HD] for base in (0, D, 2 * D)
        )
        scores = contract(queries, keys, 1, 1) * HD ** (-0.5)
        expo = jnp.exp(scores - jnp.max(scores, axis=-1, keepdims=True))
        prob = (expo / jnp.sum(expo, axis=-1, keepdims=True)).astype(bf16)
        mixed.append(contract(prob, values, 1, 0).astype(bf16))
    mixed = jnp.concatenate(mixed, axis=1)
    mixed_ref[...] = mixed
    middle = values_in + mod[2:3] * contract(mixed, out_ref[...], 1, 0)
    middle_ref[...] = middle
    normed, _ = normalize(middle)
    moe_in = (normed * (1.0 + mod[4:5]) + mod[3:4]).astype(bf16)
    tokens_out_ref[:, :D] = moe_in
    logits = contract(moe_in, router_ref[...], 1, 0)
    experts = lax.broadcasted_iota(jnp.int32, logits.shape, 1)
    chosen = [
        jnp.sum(jnp.where(ids_ref[:, j : j + 1] == experts, logits, 0.0), axis=1, keepdims=True)
        for j in range(2)
    ]
    top = jnp.maximum(chosen[0], chosen[1])
    weight = [jnp.exp(c - top) for c in chosen]
    both = weight[0] + weight[1]
    gates = [weight[0] / both, weight[1] / both]
    gates_ref[...] = jnp.concatenate(gates, axis=1)
    count = router_ref.shape[1]
    lane = lax.broadcasted_iota(jnp.int32, (1, LANES), 1)
    lane = jnp.where(lane < 3 * count, lane % count, -1)
    coded_gates = jnp.zeros((SEQ, LANES), f32)
    for j in range(2):
        coded_gates = jnp.where(ids_ref[:, j : j + 1] == lane, gates[j], coded_gates)
    tokens_out_ref[:, D:] = coded(coded_gates, lane >= 0, count)
    lane = lax.broadcasted_iota(jnp.int32, (1, LANES), 1)
    places = jnp.where(
        ids_ref[:, 0:1] == lane,
        slots_ref[:, 0:1],
        jnp.where(ids_ref[:, 1:2] == lane, slots_ref[:, 1:2], -1),
    )
    places_ref[...] = jnp.transpose(places.astype(f32))[:count].astype(jnp.int32)


def image_rows(width):
    return pl.BlockSpec((SEQ, width), lambda n: (n, 0))


def whole(*shape):
    return pl.BlockSpec(shape, lambda n: (0,) * len(shape))


def attention_call(tokens, mod, qkv, out, router, ids, slots, gates=()):
    count, experts = tokens.shape[0], router.shape[1]
    images = count // SEQ
    return pl.pallas_call(
        ordered(attention_kernel, 7, gates),
        grid=(images,),
        in_specs=[
            image_rows(D),
            pl.BlockSpec((1, 6, D), lambda n: (n, 0, 0)),
            whole(D, 3 * D),
            whole(D, D),
            whole(D, experts),
            image_rows(2),
            image_rows(2),
        ]
        + [ANYWHERE] * len(gates),
        out_specs=[
            image_rows(3 * D),
            image_rows(D),
            image_rows(D),
            image_rows(D + LANES),
            image_rows(2),
            pl.BlockSpec((experts, SEQ), lambda n: (0, n)),
        ],
        out_shape=[
            jax.ShapeDtypeStruct((count, 3 * D), bf16),
            jax.ShapeDtypeStruct((count, D), bf16),
            jax.ShapeDtypeStruct((count, D), f32),
            jax.ShapeDtypeStruct((count, D + LANES), bf16),
            jax.ShapeDtypeStruct((count, 2), f32),
            jax.ShapeDtypeStruct((experts, count), jnp.int32),
        ],
        compiler_params=pltpu.CompilerParams(vmem_limit_bytes=VMEM_LIMIT),
        cost_estimate=cost(14.0),
        name="attention_forward",
    )(tokens, mod, qkv, out, router, ids, slots, *gates)


def attention_back_kernel(
    me_ref,
    tokens_ref,
    mod_ref,
    qkv_ref,
    out_ref,
    router_ref,
    ids_ref,
    packed_ref,
    mixed_ref,
    middle_ref,
    tokens_two_ref,
    gates_ref,
    total_ref,
    other_ref,
    grad_ref,
    block_out_ref,
    grad_tokens_ref,
    grad_mod_ref,
    small_ref,
    small_send_ref,
    grad_qkv_ref,
    grad_out_ref,
    grad_router_ref,
):
    mod = mod_ref[0]
    grad = grad_ref[...].astype(f32)
    total = total_ref[...] + other_ref[...].astype(f32)
    moe = total[:, :D]
    middle = middle_ref[...]
    block_out_ref[...] = (middle + mod[5:6] * moe).astype(bf16)
    grad_gate_moe = jnp.sum(grad * moe, axis=0, keepdims=True)
    gates = gates_ref[...]
    lane = lax.broadcasted_iota(jnp.int32, (1, LANES), 1)
    lane = jnp.where(lane < 3 * router_ref.shape[1], lane % router_ref.shape[1], -1)
    dots = [
        jnp.sum(
            jnp.where(ids_ref[:, j : j + 1] == lane, total[:, 2 * D :], 0.0), axis=1, keepdims=True
        )
        for j in range(2)
    ]
    blended = gates[:, 0:1] * dots[0] + gates[:, 1:2] * dots[1]
    experts = lax.broadcasted_iota(jnp.int32, (SEQ, router_ref.shape[1]), 1)
    grad_logits = jnp.zeros((SEQ, router_ref.shape[1]), f32)
    for j in range(2):
        grad_chosen = gates[:, j : j + 1] * (dots[j] - blended)
        grad_logits += jnp.where(ids_ref[:, j : j + 1] == experts, grad_chosen, 0.0)
    grad_logits = grad_logits.astype(bf16)
    grad_in = total[:, D : 2 * D] + contract(grad_logits, router_ref[...], 1, 1)
    grad_router = contract(tokens_two_ref[:, :D], grad_logits, 0, 0)
    normed, inverse = normalize(middle)
    grad_shift_moe = jnp.sum(grad_in, axis=0, keepdims=True)
    grad_scale_moe = jnp.sum(grad_in * normed, axis=0, keepdims=True)
    grad_middle = grad + normalize_back(grad_in * (1.0 + mod[4:5]), normed, inverse)
    mixed = mixed_ref[...]
    branch = contract(mixed, out_ref[...], 1, 0)
    grad_gate_attn = jnp.sum(grad_middle * branch, axis=0, keepdims=True)
    grad_branch = (mod[2:3] * grad_middle).astype(bf16)
    grad_out = contract(mixed, grad_branch, 0, 0)
    grad_mixed = contract(grad_branch, out_ref[...], 1, 1).astype(bf16)
    packed = packed_ref[...]
    grads = [[], [], []]
    for head in range(HEADS):
        queries, keys, values = (
            packed[:, base + head * HD : base + (head + 1) * HD] for base in (0, D, 2 * D)
        )
        grad_head = grad_mixed[:, head * HD : (head + 1) * HD]
        scores = contract(queries, keys, 1, 1) * HD ** (-0.5)
        expo = jnp.exp(scores - jnp.max(scores, axis=-1, keepdims=True))
        prob = expo / jnp.sum(expo, axis=-1, keepdims=True)
        grad_prob = contract(grad_head, values, 1, 1)
        delta = jnp.sum(prob * grad_prob, axis=-1, keepdims=True)
        grad_scores = (prob * (grad_prob - delta)).astype(bf16)
        grads[0].append((contract(grad_scores, keys, 1, 0) * HD ** (-0.5)).astype(bf16))
        grads[1].append((contract(grad_scores, queries, 0, 0) * HD ** (-0.5)).astype(bf16))
        grads[2].append(contract(prob.astype(bf16), grad_head, 0, 0).astype(bf16))
    grad_packed = jnp.concatenate(grads[0] + grads[1] + grads[2], axis=1)
    normed, inverse = normalize(tokens_ref[...].astype(f32))
    attn_in = (normed * (1.0 + mod[1:2]) + mod[0:1]).astype(bf16)
    grad_qkv = contract(attn_in, grad_packed, 0, 0)
    grad_in = contract(grad_packed, qkv_ref[...], 1, 1)
    grad_shift = jnp.sum(grad_in, axis=0, keepdims=True)
    grad_scale = jnp.sum(grad_in * normed, axis=0, keepdims=True)
    grad_tokens_ref[...] = grad_middle + normalize_back(
        grad_in * (1.0 + mod[1:2]), normed, inverse
    )
    grad_mod_ref[0] = jnp.concatenate(
        [grad_shift, grad_scale, grad_gate_attn, grad_shift_moe, grad_scale_moe, grad_gate_moe],
        axis=0,
    )

    @pl.when(pl.program_id(0) == 0)
    def _():
        grad_qkv_ref[...] = grad_qkv
        grad_out_ref[...] = grad_out
        grad_router_ref[...] = grad_router

    @pl.when(pl.program_id(0) != 0)
    def _():
        grad_qkv_ref[...] += grad_qkv
        grad_out_ref[...] += grad_out
        grad_router_ref[...] += grad_router

    @pl.when(pl.program_id(0) == pl.num_programs(0) - 1)
    def _():
        columns = 2 * small_ref.shape[0]
        for j in range(columns):
            offset = me_ref[0] ^ j
            piece = jnp.concatenate(
                [
                    ref[:, j * width : (j + 1) * width]
                    for ref, width in (
                        (r, r.shape[1] // columns)
                        for r in (grad_qkv_ref, grad_out_ref, grad_router_ref)
                    )
                ]
                + [jnp.zeros((D, small_ref.shape[2] - (4 * D + router_ref.shape[1]) // columns), f32)],
                axis=1,
            )

            @pl.when((offset & 1) == 0)
            def _():
                small_ref[offset >> 1] = piece

            @pl.when((offset & 1) == 1)
            def _():
                small_send_ref[offset >> 1] = piece.astype(bf16)


def attention_back_call(
    me, columns, tokens, mod, qkv, out, router, ids, packed, mixed, middle, tokens_two, gates, total, other, grad,
    gates_on=(),
):
    count, experts = tokens.shape[0], router.shape[1]
    images = count // SEQ
    padded = -(-(4 * D + experts) // (columns * LANES)) * LANES
    mod_spec = pl.BlockSpec((1, 6, D), lambda n: (n, 0, 0))
    return pl.pallas_call(
        ordered(attention_back_kernel, 15, gates_on),
        grid=(images,),
        in_specs=[
            pl.BlockSpec(memory_space=pltpu.SMEM),
            image_rows(D),
            mod_spec,
            whole(D, 3 * D),
            whole(D, D),
            whole(D, experts),
            image_rows(2),
            image_rows(3 * D),
            image_rows(D),
            image_rows(D),
            image_rows(D + LANES),
            image_rows(2),
            image_rows(WIDE),
            image_rows(WIDE),
            image_rows(D),
        ]
        + [ANYWHERE] * len(gates_on),
        out_specs=[
            image_rows(D),
            image_rows(D),
            mod_spec,
            whole(columns // 2, D, padded),
            whole(columns // 2, D, padded),
        ],
        out_shape=[
            jax.ShapeDtypeStruct((count, D), bf16),
            jax.ShapeDtypeStruct((count, D), f32),
            jax.ShapeDtypeStruct((images, 6, D), f32),
            jax.ShapeDtypeStruct((columns // 2, D, padded), f32),
            jax.ShapeDtypeStruct((columns // 2, D, padded), bf16),
        ],
        scratch_shapes=[
            pltpu.VMEM((D, 3 * D), f32),
            pltpu.VMEM((D, D), f32),
            pltpu.VMEM((D, experts), f32),
        ],
        compiler_params=pltpu.CompilerParams(vmem_limit_bytes=VMEM_LIMIT),
        cost_estimate=cost(28.0),
        name="attention_backward",
    )(me, tokens, mod, qkv, out, router, ids, packed, mixed, middle, tokens_two, gates, total, other, grad, *gates_on)


def pack_kernel(*refs):
    refs[-1][...] = jnp.concatenate([ref[...] for ref in refs[:-1]], axis=1).astype(bf16)


def pack_call(weights):
    rows = weights[0].shape[0]
    return pl.pallas_call(
        pack_kernel,
        out_shape=jax.ShapeDtypeStruct((rows, sum(w.shape[1] for w in weights)), bf16),
        cost_estimate=cost(2.0),
        name="pack_small",
    )(*weights)


def round_kernel(up_ref, down_ref, own_ref):
    for m in range(up_ref.shape[0]):
        own_ref[2 * m] = up_ref[m].astype(bf16)
        own_ref[2 * m + 1] = down_ref[m].astype(bf16)


def round_call(up, down, gates):
    count, rows, width = up.shape
    return pl.pallas_call(
        ordered(round_kernel, 2, gates),
        in_specs=[IN_VMEM] * 2 + [ANYWHERE] * len(gates),
        out_shape=jax.ShapeDtypeStruct((2 * count, rows, width), bf16),
        cost_estimate=cost(1.5),
        name="round_experts",
    )(up, down, *gates)


def gram_of(values):
    high, middle, low = pieces_of(values)
    gram = contract(high, high, 1, 1) + contract(middle, middle, 1, 1)
    for right in (middle, low):
        term = contract(high, right, 1, 1)
        gram = gram + term + term.T
    return gram


def update_kernel(*refs, parts, moments, grams):
    out = refs[parts + moments :]
    for i in range(refs[0].shape[0]):
        grad = refs[0][i].astype(f32)
        for ref in refs[1:parts]:
            grad = grad + ref[i].astype(f32)
        which, at = i % moments, i // moments
        new = 0.5 * refs[parts + which][at] + grad
        out[which][at] = grad
        out[moments + which][at] = new
        if grams:
            out[2 * moments][i] = gram_of(new)


def update_call(parts, moments, gates, grams, name):
    stack = parts[0].shape[0]
    outs = [jax.ShapeDtypeStruct(m.shape, f32) for m in moments] * 2
    if grams:
        outs.append(jax.ShapeDtypeStruct((stack, D, D), f32))
    return pl.pallas_call(
        ordered(
            functools.partial(update_kernel, parts=len(parts), moments=len(moments), grams=grams),
            len(parts) + len(moments),
            gates,
        ),
        in_specs=[IN_VMEM] * (len(parts) + len(moments)) + [ANYWHERE] * len(gates),
        out_shape=outs,
        compiler_params=pltpu.CompilerParams(vmem_limit_bytes=VMEM_LIMIT),
        cost_estimate=cost(4.0 if grams else 2.0),
        name=name,
    )(*parts, *moments, *gates)


def arrange_kernel(me_ref, even_ref, odd_ref, out_ref):
    rows = even_ref.shape[2]
    for odd, ref in enumerate((even_ref, odd_ref)):
        for i in range(ref.shape[0]):
            at = pl.multiple_of((me_ref[0] ^ (2 * i + odd)) * rows, 8)
            out_ref[:, pl.ds(at, rows), :] = ref[i]


def arrange_call(me, even, odd):
    count, stack, rows, width = even.shape
    return pl.pallas_call(
        arrange_kernel,
        in_specs=[pl.BlockSpec(memory_space=pltpu.SMEM), IN_VMEM, IN_VMEM],
        out_shape=jax.ShapeDtypeStruct((stack, 2 * count * rows, width), even.dtype),
        compiler_params=pltpu.CompilerParams(vmem_limit_bytes=VMEM_LIMIT),
        cost_estimate=cost(3.0),
        name="arrange_rows",
    )(me, even, odd)


def modulation_kernel(
    me_ref, vectors_ref, moments_ref, grad_ref, gram_ref, columns_ref, *, columns
):
    width = moments_ref.shape[1]
    cond = vectors_ref[:, columns * width :].astype(bf16)
    cond = jnp.concatenate([cond] * 3, axis=0)
    for j in range(columns):

        @pl.when(me_ref[1] == j)
        def _():
            vectors = pieces_of(vectors_ref[:, j * width : (j + 1) * width])
            grad = contract(cond, jnp.concatenate(vectors, axis=0), 0, 0)
            grad_ref[...] = grad
            columns_ref[...] = 0.5 * moments_ref[...] + grad

    gram_ref[...] = gram_of(columns_ref[...])


def modulation_call(me, vectors, moments, columns, gates):
    width = moments.shape[1]
    return pl.pallas_call(
        ordered(functools.partial(modulation_kernel, columns=columns), 3, gates),
        in_specs=[pl.BlockSpec(memory_space=pltpu.SMEM)]
        + [IN_VMEM] * 2
        + [ANYWHERE] * len(gates),
        out_shape=[
            jax.ShapeDtypeStruct((D, width), f32),
            jax.ShapeDtypeStruct((D, D), f32),
            jax.ShapeDtypeStruct((D, width), f32),
        ],
        compiler_params=pltpu.CompilerParams(vmem_limit_bytes=2 * VMEM_LIMIT),
        cost_estimate=cost(4.0),
        name="modulation_update",
    )(me, vectors, moments, *gates)


def assemble_kernel(*refs, layout, cuts):
    me_ref, cond_ref, grad_ref = refs[:3]
    pieces = refs[3 : 3 + len(layout)]
    full_refs = refs[3 + len(layout) : 7 + len(layout)]
    mod_ref, grads_ref, buffer, sem = refs[7 + len(layout) :]
    rows = pieces[0].shape[1]
    copies = []
    for ref, (odd, column, start) in zip(pieces, layout, strict=True):
        for i in range(ref.shape[0]):
            at = (me_ref[0] ^ (2 * (start + i) + odd)) * rows
            copies.append(
                pltpu.make_async_copy(
                    ref.at[i],
                    buffer.at[me_ref[1] ^ column, pl.ds(pl.multiple_of(at, 16), rows), :],
                    sem.at[len(copies)],
                )
            )
    for copy in copies:
        copy.start()
    for copy in copies:
        copy.wait()
    for ref, start, end in zip(full_refs, cuts[:-1], cuts[1:], strict=True):
        ref[...] = jnp.concatenate(
            [buffer[j, :, start:end] for j in range(buffer.shape[0])], axis=1
        )
    mod = contract(cond_ref[...], full_refs[0][...], 1, 0)
    for i in range(6):
        mod_ref[:, i, :] = mod[:, i * D : (i + 1) * D]
    for n in range(mod.shape[0]):
        at = slice(n * SEQ, (n + 1) * SEQ)
        grads_ref[at] = (mod[n : n + 1, 5 * D :] * grad_ref[at].astype(f32)).astype(bf16)


def assemble_call(me, cond, grad, pieces, layout, cuts, columns):
    images, count = cond.shape[0], grad.shape[0]
    return pl.pallas_call(
        functools.partial(assemble_kernel, layout=layout, cuts=cuts),
        in_specs=[pl.BlockSpec(memory_space=pltpu.SMEM), IN_VMEM, IN_VMEM]
        + [ANYWHERE] * len(pieces),
        out_shape=[
            jax.ShapeDtypeStruct((D, columns * (end - start)), bf16)
            for start, end in zip(cuts[:-1], cuts[1:], strict=True)
        ]
        + [
            jax.ShapeDtypeStruct((images, 6, D), f32),
            jax.ShapeDtypeStruct((count, D), bf16),
        ],
        scratch_shapes=[
            pltpu.VMEM((columns, D, cuts[-1]), bf16),
            pltpu.SemaphoreType.DMA((sum(p.shape[0] for p in pieces),)),
        ],
        compiler_params=pltpu.CompilerParams(vmem_limit_bytes=VMEM_LIMIT),
        cost_estimate=cost(5.0),
        name="assemble_small",
    )(me, cond, grad, *pieces)


def product(left, right, parts):
    left, right = pieces_of(left), pieces_of(right)
    terms = ((0, 0), (0, 1), (1, 0), (0, 2), (2, 0), (1, 1))[: 6 if parts == 3 else 3]
    return contract(
        jnp.concatenate([left[i] for i, _ in terms], axis=1),
        jnp.concatenate([right[j] for _, j in terms], axis=0),
        1,
        0,
    )


def polish_kernel(gram_ref, mixer_ref):
    count, size, _ = gram_ref.shape
    identity = lax.broadcasted_iota(jnp.int32, (size, size), 0) == lax.broadcasted_iota(
        jnp.int32, (size, size), 1
    )
    state = []
    for i in range(count):
        gram = gram_ref[i]
        squares = jnp.sum(jnp.where(identity, gram, 0.0), axis=(0, 1), keepdims=True)
        scale = 1.0 / (jnp.sqrt(squares) + 1e-07)
        state.append((gram * (scale * scale), None, scale))
    for step in range(NS_STEPS):
        parts = 3 if step < 2 else 2
        after_step = []
        for gram, mixer, scale in state:
            poly = cubic_term * gram + quintic_term * product(gram, gram, parts)
            poly = jnp.where(identity, linear_term + poly, poly)
            if step == NS_STEPS - 1:
                mixer = product(poly, mixer, parts)
            elif step == 0:
                mixer, gram = poly, product(poly, product(gram, poly, parts), parts)
            else:
                both = jnp.concatenate([product(gram, poly, parts), mixer], axis=1)
                both = product(poly, both, parts)
                gram, mixer = both[:, :size], both[:, size:]
            after_step.append((gram, mixer, scale))
        state = after_step
    for i in range(count):
        mixer_ref[i] = state[i][1] * state[i][2]


def polish_call(grams, name, gates=()):
    count, size, _ = grams.shape
    return pl.pallas_call(
        ordered(polish_kernel, 1, gates),
        in_specs=[IN_VMEM] + [ANYWHERE] * len(gates),
        out_shape=jax.ShapeDtypeStruct(grams.shape, f32),
        compiler_params=pltpu.CompilerParams(vmem_limit_bytes=VMEM_LIMIT),
        cost_estimate=cost(13.0 * count if size > 128 else 4.0),
        name=name,
    )(grams, *gates)


def stacked_precise(left, right, left_dim, right_dim):
    return lax.dot_general(
        left,
        right,
        (((left_dim,), (right_dim,)), ((0,), (0,))),
        precision=lax.Precision.HIGHEST,
        preferred_element_type=f32,
    )


def on_device(
    tokens_in,
    condition,
    grad_output,
    expert_ids,
    slot_rows,
    expert_counts,
    ada_weight,
    ada_moment,
    qkv_weight,
    qkv_moment,
    out_weight,
    out_moment,
    router_weight,
    router_moment,
    shared_up,
    shared_up_moment,
    shared_down,
    shared_down_moment,
    expert_up,
    expert_up_moment,
    expert_down,
    expert_down_moment,
):
    count = tokens_in.shape[0]
    images = count // SEQ
    nb, nd = lax.axis_size("blk"), lax.axis_size("dp")
    blk, dp = lax.axis_index("blk"), lax.axis_index("dp")
    blk_masks = bits("blk")[1:] + [1]
    dp_masks = bits("dp")
    col_masks = [m for m in dp_masks if m != TP]
    high_masks = [m for m in dp_masks if m not in (1, TP)]
    height = ada_weight.shape[0]
    wide_ada, wide_qkv, wide_out, wide_router = (
        w.shape[1] for w in (ada_weight, qkv_weight, out_weight, router_weight)
    )
    cuts = (0, wide_ada, wide_ada + wide_qkv, wide_ada + wide_qkv + wide_out)

    me = jnp.stack([blk, dp]).astype(jnp.int32)
    half = nb // 4

    def over_z(own):
        return jnp.stack([own] + [swap(own, "blk", 2 * k) for k in range(1, nb // 2)])

    def collect(own):
        even = over_z(own)
        return arrange_call(me, even, swap(even, "blk", 1))

    cond_low = jax.nn.silu(condition).astype(bf16)
    small = over_z(pack_call((ada_weight, qkv_weight, out_weight, router_weight)))
    small_x, small_y = swap(small, "blk", 1), swap(small, "dp", TP)
    pieces = [
        (small, 0, 0, 0),
        (small_x, 1, 0, 0),
        (small_y, 0, TP, 0),
        (swap(small_y[:half], "blk", 1), 1, TP, 0),
        (swap(small_x[half:], "dp", TP), 1, TP, half),
    ]
    for mask in high_masks + [1]:
        pieces = pieces + [
            (swap(piece, "dp", mask), odd, column ^ mask, start)
            for piece, odd, column, start in pieces
        ]
    ada_full, qkv_full, out_full, router_full, modulation, grad_moe = assemble_call(
        me,
        cond_low,
        grad_output,
        [p[0] for p in pieces],
        [p[1:] for p in pieces],
        cuts + (cuts[-1] + wide_router,),
        nd,
    )

    def other_half(own):
        for mask in high_masks[::-1]:
            own = jnp.concatenate([own, swap(own, "dp", mask)], axis=-1)
        return own, swap(own, "dp", 1)

    shared_even = over_z(round_call(shared_up, shared_down, (pieces[3][0], pieces[4][0])))
    shared = arrange_call(me, shared_even, swap(shared_even, "blk", 1))
    expert_own = round_call(expert_up, expert_down, (shared_even,))
    shared = shared.reshape(SHARED, 2, D, -1)
    shared_own, shared_other = other_half(shared)

    def parent(k):
        return k & (k - 1)

    def over_bit(values, k):
        return swap(values, "blk", 2 * (k & -k))

    firsts = {0: expert_own, 1: over_bit(expert_own, 1)}
    for k in sorted(range(2, nb // 2), key=lambda k: (k.bit_count(), -k)):
        firsts[k] = over_bit(firsts[parent(k)], k)
    pairs = {k: other_half(f) + other_half(swap(f, "blk", 1)) for k, f in firsts.items()}

    def everywhere(rows):
        rows = over_z(rows)
        rows_x, rows_y = swap(rows, "blk", 1), swap(rows, "dp", TP)
        rows = jnp.concatenate(
            [rows, rows_x, rows_y, swap(rows_y[:half], "blk", 1), swap(rows_x[half:], "dp", TP)]
        )
        for mask in high_masks + [1]:
            rows = jnp.concatenate([rows, swap(rows, "dp", mask)])
        return rows.reshape(-1, rows.shape[-1])

    ada_even = over_z(ada_moment[None])
    ada_moments = arrange_call(me, ada_even, swap(ada_even, "blk", 1))[0]

    block_count = (expert_counts[0] + BLOCK - 1) // BLOCK
    block_first = jnp.cumsum(block_count) - block_count
    blocks = jnp.stack([block_first, block_count], axis=1)
    blocks = jnp.concatenate([blocks, swap(blocks, "dp", TP)], axis=1)

    partner_grads = swap(grad_moe, "dp", TP)
    packed, mixed, middle, tokens_two, gates, places = attention_call(
        tokens_in,
        modulation,
        qkv_full,
        out_full,
        router_full,
        expert_ids,
        slot_rows,
    )
    places = (places, swap(places, "dp", TP))
    tokens_pair = (tokens_two, swap(tokens_two, "dp", TP))
    grads_pair = (grad_moe, partner_grads)

    def merge(keep, send):
        grads = keep + swap(send, "dp", 1).astype(f32)
        for mask in high_masks:
            half = grads.shape[-1] // 2
            got = swap(grads[..., half:].astype(bf16), "dp", mask)
            grads = grads[..., :half] + got.astype(f32)
        return grads

    def over_x(grads):
        return grads[0] + swap(grads[1].astype(bf16), "blk", 1).astype(f32)

    def over_x(grads):
        return grads[0] + swap(grads[1].astype(bf16), "blk", 1).astype(f32)

    def from_z(grads, k):
        return swap(grads.astype(bf16), "blk", 2 * k).astype(f32)

    def shared_over_x(grads):
        def piece(offset):
            return lax.dynamic_slice_in_dim(grads, (blk ^ offset) * height, height, 2)

        return over_x([jnp.stack([piece(j) for j in range(o, nb, 2)]) for o in range(2)])

    def routed(k, totals, last=False, gates=()):
        table = []
        for r in (2 * k, 2 * k + 1):
            line = lax.dynamic_index_in_dim(blocks, blk ^ r, 0, False)
            table.append(jnp.concatenate([line, (blk ^ r)[None]]))
        total, total_two, keep, send = routed_call(
            jnp.stack(table), tokens_pair, grads_pair, places, pairs[k], totals, last, gates
        )
        return (total, total_two), merge(keep, send)

    total, sums = shared_first_call(
        (tokens_pair[0], grads_pair[0]), shared_own, shared_other, gates=(partner_grads, ada_even, pairs[2][0])
    )
    order = [1] + list(range(2, nb // 2))[::-1] + [0]
    sums_of = {}

    def halve_x(step):
        k = order[step]
        terms = [merged[step][0], swap(merged[step][1].astype(bf16), "blk", 1)]
        terms = terms + [sums_of[c] for c in range(k + 1, nb // 2) if parent(c) == k]
        if k:
            terms = sum(t.astype(f32) for t in terms)
            sums_of[k] = over_bit(terms.astype(bf16), k)
        return terms

    totals, merged_one = routed(
        order[0], (total, jnp.zeros(total.shape, f32)), gates=(pairs[3][0],)
    )
    total_two, keep, send = shared_second_call(
        (tokens_pair[1], grads_pair[1]), shared_own, shared_other, sums, totals[1], gates=(ada_moments, pairs[2][2], pairs[3][2])
    )
    totals = (totals[0], total_two)
    merged = [merged_one]
    shared_merged = merge(keep, send)
    for step, k in enumerate(order[1:], 1):
        if step == 1:
            waits = [merged[0]]
        elif step == 2:
            waits = [shared_merged, halve_x(0)[0]]
        else:
            waits = [merged[step - 2]]
            if step == 3:
                shared_halved = shared_over_x(shared_merged)
                waits.append(shared_halved)
            else:
                halve_x(step - 3)
        totals, more = routed(k, totals, step == len(order) - 1, waits)
        merged.append(more)
    for step in range(len(order) - 3, len(order)):
        expert_terms = halve_x(step)
    shared_terms = [shared_halved[0]]
    for k in range(1, nb // 2):
        shared_terms.append(swap(shared_halved[k].astype(bf16), "blk", 2 * k))
    shared_terms = [t.reshape((2 * SHARED,) + t.shape[2:]) for t in shared_terms]
    shared_up_grad, shared_down_grad, shared_up_moment_new, shared_down_moment_new = update_call(
        shared_terms, (shared_up_moment, shared_down_moment), totals[1:], False, "shared_update"
    )

    other = swap(totals[1], "dp", TP)

    block_out, grad_tokens, grad_mod, small_grads, small_send = attention_back_call(
        me[1:],
        nd,
        tokens_in,
        modulation,
        qkv_full,
        out_full,
        router_full,
        expert_ids,
        packed,
        mixed,
        middle,
        tokens_two,
        gates,
        totals[0],
        other,
        grad_output,
        gates_on=(shared_up_grad,),
    )
    grad_mod = grad_mod.reshape(images, 6 * D)
    grad_silu = precise(grad_mod, ada_full.astype(f32), 1, 1)
    grad_condition = jax.vjp(jax.nn.silu, condition)[1](grad_silu)[0]

    small_grads = small_grads + swap(small_send, "dp", 1).astype(f32)
    for mask in [m for m in dp_masks[::-1] if m != 1]:
        part = small_grads.shape[0] // 2
        got = swap(small_grads[part:].astype(bf16), "dp", mask)
        small_grads = small_grads[:part] + got.astype(f32)
    small_grads = scatter_blk(by_offset(small_grads[0].reshape(nb, height, -1), "blk"))
    small_cuts = (0, wide_qkv, wide_qkv + wide_out)
    qkv_grad = small_grads[:, : small_cuts[1]]
    out_grad = small_grads[:, small_cuts[1] : small_cuts[2]]
    router_grad = small_grads[:, small_cuts[2] : small_cuts[2] + wide_router]

    core = dp & 1

    def halve(stack):
        half = stack.shape[0] // 2
        mine = jnp.where(core == 0, stack[:half], stack[half:])
        theirs = jnp.where(core == 0, stack[half:], stack[:half])
        return mine + swap(theirs, "dp", 1)

    def join(mine):
        theirs = swap(mine, "dp", 1)
        return jnp.concatenate(
            [jnp.where(core == 0, mine, theirs), jnp.where(core == 0, theirs, mine)]
        )

    upper = (dp & TP) != 0

    def deal(gram):
        gram = halve(gram)
        sent = jnp.where(upper, gram[:1], gram[1:])
        gram = jnp.where(upper, gram[1:], gram[:1]) + swap(sent, "dp", TP)
        for mask in high_masks:
            gram = gram + swap(gram, "dp", mask)
        return gram, sent

    def gather(mine):
        theirs = swap(mine, "dp", TP)
        return join(
            jnp.concatenate([jnp.where(upper, theirs, mine), jnp.where(upper, mine, theirs)])
        )

    shared_new = jnp.concatenate([shared_up_moment_new, shared_down_moment_new])
    shared_cols = jnp.swapaxes(lax.all_gather(shared_new, "blk"), 0, 1)
    shared_cols = shared_cols.reshape(2 * SHARED, D, -1)
    shared_gram, _ = deal(stacked_precise(shared_cols, shared_cols, 2, 2))

    vectors = everywhere(jnp.concatenate([grad_mod, cond_low.astype(f32)], axis=1))
    ada_grad_cols, ada_gram, ada_cols = modulation_call(
        me, vectors, ada_moments, nd, (shared_cols,)
    )

    def own_block(matrix, width):
        return lax.dynamic_slice(matrix, (blk * height, dp * width), (height, width))

    def own_rows(stack):
        return lax.dynamic_slice_in_dim(stack, blk * height, height, stack.ndim - 2)

    ada_grad = own_rows(ada_grad_cols)

    expert_up_grad, expert_down_grad, expert_up_moment_new, expert_down_moment_new, expert_gram = (
        update_call(
            expert_terms, (expert_up_moment, expert_down_moment), (grad_tokens,), True, "expert_update"
        )
    )
    ada_moment_new = 0.5 * ada_moment + ada_grad
    qkv_moment_new = 0.5 * qkv_moment + qkv_grad
    out_moment_new = 0.5 * out_moment + out_grad
    router_moment_new = 0.5 * router_moment + router_grad

    small_new = jnp.concatenate([qkv_moment_new, out_moment_new, router_moment_new], axis=1)
    small_cols = collect(small_new[None])[0]
    qkv_cols = small_cols[:, : small_cuts[1]]
    out_cols = small_cols[:, small_cuts[1] : small_cuts[2]]
    router_cols, offsets = double(small_cols[:, small_cuts[2] :].T, "dp", dp_masks)
    router_whole = in_order(router_cols, offsets, "dp").reshape(-1, D)
    gram = [precise(qkv_cols, qkv_cols, 1, 1), precise(out_cols, out_cols, 1, 1), ada_gram]
    dense_gram, dense_sent = deal(jnp.stack(gram + [jnp.zeros((D, D), f32)]))

    mine = polish_call(shared_gram, "polish_shared", (dense_sent,))
    shared_mixer = gather(mine)
    gram = halve(expert_gram)
    for mask in [TP] + high_masks:
        gram = gram + swap(gram, "dp", mask)
    solved = polish_call(gram, "polish_experts", (mine,))
    expert_new = jnp.concatenate([expert_up_moment_new, expert_down_moment_new])
    orth_expert = stacked_precise(join(solved), expert_new, 2, 1)
    orth_shared = stacked_precise(own_rows(shared_mixer), shared_cols, 2, 1)
    orth_shared_up, orth_shared_down = orth_shared[:SHARED], orth_shared[SHARED:]

    mixer = gather(polish_call(dense_gram, "polish_dense", (solved,)))
    ada_mixer = mixer[2]
    orth_ada = precise(own_rows(ada_mixer), ada_cols)
    orth_qkv = precise(own_rows(mixer[0]), qkv_cols)
    orth_out = precise(own_rows(mixer[1]), out_cols)
    experts = router_whole.shape[0]
    router_gram = jnp.pad(
        precise(router_whole, router_whole, 1, 1), ((0, 128 - experts), (0, 128 - experts))
    )
    router_mixer = polish_call(router_gram[None], "polish_router")[0, :experts, :experts]
    orth_router = own_block(precise(router_whole, router_mixer, 0, 1), wide_router)

    ada_new = ada_weight - math.sqrt(6.0) * orth_ada
    qkv_new = qkv_weight - math.sqrt(3.0) * orth_qkv
    out_new = out_weight - math.sqrt(D / (D // 64)) * orth_out
    router_new = router_weight - 0.5 * orth_router
    shared_up_new = shared_up - math.sqrt(FF / D) * orth_shared_up
    shared_down_new = shared_down - 1.0 * orth_shared_down
    expert_up_new = expert_up - math.sqrt(FF / D) * orth_expert[0:1]
    expert_down_new = expert_down - 1.0 * orth_expert[1:2]
    return (
        block_out,
        grad_tokens,
        grad_condition,
        ada_grad,
        ada_moment_new,
        ada_new,
        ada_new.astype(bf16),
        qkv_grad,
        qkv_moment_new,
        qkv_new,
        qkv_new.astype(bf16),
        out_grad,
        out_moment_new,
        out_new,
        out_new.astype(bf16),
        router_grad,
        router_moment_new,
        router_new,
        router_new.astype(bf16),
        shared_up_grad,
        shared_up_moment_new,
        shared_up_new,
        shared_up_new.astype(bf16),
        shared_down_grad,
        shared_down_moment_new,
        shared_down_new,
        shared_down_new.astype(bf16),
        expert_up_grad,
        expert_up_moment_new,
        expert_up_new,
        expert_up_new.astype(bf16),
        expert_down_grad,
        expert_down_moment_new,
        expert_down_new,
        expert_down_new.astype(bf16),
    )


def solution(mesh):
    tokens = P(("blk", "dp"), None)
    dense = P("blk", "dp")
    shared = P(None, "blk", "dp")
    routed = P("blk", None, "dp")
    in_specs = (tokens,) * 6 + (dense,) * 8 + (shared,) * 4 + (routed,) * 4
    out_specs = (tokens,) * 3 + (dense,) * 16 + (shared,) * 8 + (routed,) * 8
    return jax.shard_map(
        on_device, mesh=mesh, in_specs=in_specs, out_specs=out_specs, check_vma=False
    )
```
